256 devices in a mesh: sample: 16 (over z, core), gene: 16 (over y, x).
Axes of the slice: x: 4, y: 4, z: 8, core: 2. Of those that a mesh axis runs over, the one named last changes fastest.
Arguments:
- samples: bfloat16 [2560, 65536], P('sample', 'gene'), may hold values from -6 to 6
- diag_tiles: float32 [512, 128, 128], P('gene')
- cross_tiles: float32 [16, 16, 2, 128, 128], P('gene'), may hold values from -0.3 to 0.3
- peer_cols: int32 [16, 16, 2], P('gene'), may hold values from 0 to 1, as said below
- pair_counts: int32 [16, 16], P('gene'), may hold values from 0 to 2, as said below
Outputs:
- precision_diag: float32 [512, 128, 128], P('gene')
- precision_cross: float32 [16, 16, 2, 128, 128], P('gene')
The draws below stay inside these ranges and needn't reach their ends.
Inputs may be any that keep to these rules, and one draw needn't show every extreme that they name: peer_cols[h, g, p] is the row block, within the blocks of index h, of cross tile g, h, p; for each g and h the live tiles p < pair_counts[g, h] are distinct tiles. Only the first 2 blocks of each index take part in cross tiles. pair_counts is symmetric and zero where g equals h.
All inputs are finite; a program needn't handle non-finite values.
Results may differ from the reference program's by a relative error of at most 0.0025.
Values may be sent and summed in bfloat16 or wider, within the bound.
No kernel may reach another device: no remote copies, remote signals or barrier semaphores. Data moves between devices by JAX's collectives and lax.ppermute only.
A program may use at most 64 MiB of HBM per device.

```python
import jax
import jax.numpy as jnp
from jax import lax

BLK = 128
BLK_DEV = 32
HUBS = 2
PEER = 2
ITERS = 2
GENE_BLOCKS = 512
GENES = 65536
SAMPLES = 2560
N_GENE = 16


def pattern_tables(key):
    key_counts, key_base, key_rows = jax.random.split(jax.random.fold_in(key, 17), 3)
    upper = jax.random.randint(key_counts, (N_GENE, N_GENE), 0, PEER + 1)
    row_ids = lax.broadcasted_iota(jnp.int32, (N_GENE, N_GENE), 0)
    col_ids = lax.broadcasted_iota(jnp.int32, (N_GENE, N_GENE), 1)
    upper = jnp.where((row_ids == 0) & (col_ids == 1), PEER, upper)
    counts = jnp.where(row_ids < col_ids, upper, jnp.where(row_ids > col_ids, upper.T, 0)).astype(jnp.int32)
    base = jax.random.randint(key_base, (N_GENE, N_GENE, 1), 0, HUBS)
    slot_ids = lax.broadcasted_iota(jnp.int32, (N_GENE, N_GENE, PEER), 2)
    first_side = (base + slot_ids) % HUBS
    second_side = jax.random.randint(key_rows, (N_GENE, N_GENE, PEER), 0, HUBS)
    above = (row_ids < col_ids)[:, :, None]
    columns = jnp.where(above, first_side, jnp.transpose(second_side, (1, 0, 2))).astype(jnp.int32)
    return (columns, counts)


def draw_peer_cols(key, part):
    columns, counts = pattern_tables(key)
    return columns


def draw_pair_counts(key, part):
    columns, counts = pattern_tables(key)
    return counts


def draw_diag_tiles(key, part):
    key_off, key_diag = jax.random.split(jax.random.fold_in(key, 11))
    shape = (GENE_BLOCKS, BLK, BLK)
    off_part = 0.05 * jax.random.normal(key_off, shape, jnp.float32)
    diag_part = jax.random.uniform(key_diag, (GENE_BLOCKS, BLK, 1), jnp.float32, 0.8, 1.6)
    on_diagonal = lax.broadcasted_iota(jnp.int32, shape, 1) == lax.broadcasted_iota(jnp.int32, shape, 2)
    return jnp.where(on_diagonal, diag_part, off_part).astype(jnp.float32)


def steps_of(own_key, shape, shards, smallest, largest):
    gain, own = 1.0, jax.random.fold_in(own_key, 6)
    for axis_at, blocks in shards:
        heights = jnp.exp(jax.random.uniform(jax.random.fold_in(own, axis_at), (blocks,), jnp.float32, smallest / len(shards), largest / len(shards)))
        gain = gain * jnp.repeat(heights, shape[axis_at] // blocks).reshape([-1 if axis == axis_at else 1 for axis in range(len(shape))])
    return gain


def centred(rng, shape, deviation, most, shards=(), held_as=jnp.bfloat16):
    values = jax.random.normal(rng, shape, jnp.float32) * deviation
    if len(shards) > 0:
        values = steps_of(rng, shape, shards, -0.22, 0.18) * values
    return jnp.clip(values, min=-most, max=most).astype(held_as)


def setup_inputs(seed: int = 0) -> dict:
    splits = jax.random.split(jax.random.key(seed), 6)
    samples = centred(splits[0], (SAMPLES, GENES), 1.0, 6.0, ((0, 16), (1, 16)))
    diag_tiles = draw_diag_tiles(jax.random.fold_in(splits[5], 71), 0)
    cross_tiles = centred(splits[2], (N_GENE, N_GENE, PEER, BLK, BLK), 0.05, 0.3, ((0, 16),), jnp.float32)
    peer_cols = draw_peer_cols(jax.random.fold_in(splits[5], 71), 0)
    pair_counts = draw_pair_counts(jax.random.fold_in(splits[5], 71), 0)
    return {"samples": samples, "diag_tiles": diag_tiles, "cross_tiles": cross_tiles, "peer_cols": peer_cols, "pair_counts": pair_counts}


step_length = 0.5
shrinkage = 0.02

def proximal(tiles, gradient, on_diagonal, keep_mask):
    stepped = tiles - step_length * gradient
    barrier = 0.5 * (stepped + jnp.sqrt(stepped * stepped + 4.0 * step_length))
    shrunk = jnp.sign(stepped) * jnp.maximum(jnp.abs(stepped) - shrinkage, 0.0)
    return jnp.where(on_diagonal, barrier, shrunk) * keep_mask

def rounded(tiles):
    lowered = tiles.astype(jnp.bfloat16)
    lowered = lax.optimization_barrier(lowered)
    return lowered.astype(jnp.float32)

def reference(samples, diag_tiles, cross_tiles, peer_cols, pair_counts):
    block_view = samples.reshape(SAMPLES, GENE_BLOCKS, BLK)
    live_mask = (jnp.arange(PEER, dtype=jnp.int32)[None, None, :] < pair_counts[:, :, None]).astype(jnp.float32)
    owners = jnp.arange(N_GENE, dtype=jnp.int32)
    row_global = (owners[None, :, None] * BLK_DEV + jnp.transpose(peer_cols, (1, 0, 2))).astype(jnp.int32)
    diagonal_mask = jnp.eye(BLK, dtype=bool)
    estimate_diag = diag_tiles
    estimate_cross = cross_tiles * live_mask[:, :, :, None, None]
    for iteration in range(ITERS):
        lowered_diag = rounded(estimate_diag)
        lowered_cross = rounded(estimate_cross)

        def one_holder(holder):
            start_block = (holder * BLK_DEV).astype(jnp.int32)
            own_blocks = lax.dynamic_slice_in_dim(block_view, start_block, BLK_DEV, 1).astype(jnp.float32)
            row_blocks = jnp.take(block_view, row_global[holder], axis=1).astype(jnp.float32)
            holder_diag = lax.dynamic_slice_in_dim(lowered_diag, start_block, BLK_DEV, 0)
            local_part = jnp.einsum('scb,cbd->scd', own_blocks, holder_diag)
            remote = jnp.einsum('shpb,hpbd->shpd', row_blocks, lowered_cross[holder])
            column_hot = (peer_cols[holder][:, :, None] == jnp.arange(BLK_DEV, dtype=jnp.int32)[None, None, :]).astype(jnp.float32) * live_mask[holder][:, :, None]
            columns = local_part + jnp.einsum('shpd,hpc->scd', remote, column_hot, precision=lax.Precision.HIGHEST)
            projected = rounded(columns)
            grad_diag = jnp.einsum('scb,scd->cbd', own_blocks, projected) / SAMPLES
            picked = jnp.take(projected, peer_cols[holder], axis=1)
            grad_cross = jnp.einsum('shpb,shpd->hpbd', row_blocks, picked) / SAMPLES
            return (grad_diag, grad_cross)
        grad_diag, grad_cross = lax.map(one_holder, owners)
        grad_diag = grad_diag.reshape(GENE_BLOCKS, BLK, BLK)
        symmetric_diag = 0.5 * (grad_diag + jnp.swapaxes(grad_diag, 1, 2))
        symmetric_cross = 0.5 * (grad_cross + jnp.swapaxes(jnp.transpose(grad_cross, (1, 0, 2, 3, 4)), 3, 4))
        estimate_diag = proximal(estimate_diag, symmetric_diag, diagonal_mask[None], 1.0)
        estimate_cross = proximal(estimate_cross, symmetric_cross, False, live_mask[:, :, :, None, None])
    return (estimate_diag, estimate_cross)
```

```python
import functools

import jax
import jax.numpy as jnp
from jax import lax
from jax.experimental import pallas as pl
from jax.experimental.pallas import tpu as pltpu
from jax.sharding import PartitionSpec as P

ITERS = 2
STEP = 0.5
SHRINK = 0.02
TILE = 128
BF = jnp.bfloat16
F32 = jnp.float32

BACK = (0, 1, -1, 2, -2, 3, -3, 4)
ORDER = tuple((back, other) for other in (0, 1) for back in BACK)

VMEM = pl.BlockSpec(memory_space=pltpu.VMEM)
SMEM = pl.BlockSpec(memory_space=pltpu.SMEM)
PARAMS = pltpu.CompilerParams(vmem_limit_bytes=48 * 1024 * 1024)


def shift_z(x, chips):
    count = lax.axis_size("sample")
    return lax.ppermute(x, "sample", [(i, (i + 2 * chips) % count) for i in range(count)])


def swap_core(x):
    count = lax.axis_size("sample")
    return lax.ppermute(x, "sample", [(i, i ^ 1) for i in range(count)])


def ring_gather(x):
    half = x.shape[0] // 2
    up = down = x
    own = [x]
    for _ in range(3):
        up, down = shift_z(up, 1), shift_z(down, -1)
        own += [up, down]
    far = jnp.concatenate([shift_z(up[:half], 1), shift_z(down[half:], -1)], axis=0)
    own.append(far)
    return own + [swap_core(piece) for piece in own]


def mirror(x):
    samples, genes = lax.axis_size("sample"), lax.axis_size("gene")
    pairs = [(s * genes + g, s * genes + (g ^ s)) for s in range(samples) for g in range(genes)]
    return lax.ppermute(x, ("sample", "gene"), pairs)


def dot(a, b):
    return jnp.dot(a, b, preferred_element_type=F32)


def dot_over_rows(a, b):
    return lax.dot_general(a, b, (((0,), (0,)), ((), ())), preferred_element_type=F32)


def placed(tiles, code_ref, at):
    zero = jnp.zeros((TILE, TILE), BF)
    rows = []
    for p in range(2):
        tile = tiles[p].astype(BF)
        rows.append(
            jnp.concatenate(
                [jnp.where(code_ref[at, p] == c, tile, zero) for c in range(2)], axis=1
            )
        )
    return jnp.concatenate(rows, axis=0)


def first_columns_kernel(code_ref, me_ref, slots_ref, cross_ref, hub_ref, y_ref):
    total = jnp.zeros(y_ref.shape, F32)
    for h in range(cross_ref.shape[0]):
        own = me_ref[0] == h
        tiles = [jnp.where(own, hub_ref[p], cross_ref[h, p]) for p in range(2)]
        total += dot(slots_ref[h], placed(tiles, code_ref, h))
    y_ref[...] = total.astype(BF)


def later_columns_kernel(code_ref, peer_ref, slots_ref, *refs):
    pieces, y_ref = refs[:-1], refs[-1]
    total = jnp.zeros(y_ref.shape, F32)
    for j, piece in enumerate(pieces):
        total += dot(slots_ref[peer_ref[j]], placed([piece[0], piece[1]], code_ref, j))
    y_ref[...] = total.astype(BF)


def gradient_kernel(code_ref, rows_ref, *refs):
    pieces, out_ref = refs[:-1], refs[-1]
    total = jnp.zeros((2 * TILE, 2 * TILE), F32)
    for j, piece in enumerate(pieces):
        total += dot_over_rows(rows_ref[j], piece[...])
    for p in range(2):
        rows = total[p * TILE : (p + 1) * TILE]
        out_ref[p] = jnp.where(code_ref[p] == 1, rows[:, TILE:], rows[:, :TILE])


def proximal(tile, gradient, mirrored, diagonal, sample_total):
    symmetric = 0.5 * (gradient + mirrored.T) / sample_total
    stepped = tile - STEP * symmetric
    shrunk = jnp.where(
        stepped > 0, jnp.maximum(stepped - SHRINK, 0.0), jnp.minimum(stepped + SHRINK, 0.0)
    )
    barrier = 0.5 * (stepped + jnp.sqrt(stepped * stepped + 4.0 * STEP))
    return jnp.where(diagonal, barrier, shrunk)


def eye():
    shape = (TILE, TILE)
    return lax.broadcasted_iota(jnp.int32, shape, 0) == lax.broadcasted_iota(jnp.int32, shape, 1)


def step_kernel(sample_total, code_ref, place_ref, tile_ref, grad_ref, mirrored_ref, new_ref, low_ref):
    is_hub = place_ref[0] == 0
    on_diagonal = jnp.where(is_hub, eye().astype(F32), 0.0) > 0.5
    for p in range(2):
        new = proximal(tile_ref[p], grad_ref[p], mirrored_ref[p], on_diagonal, sample_total)
        new = jnp.where(code_ref[p] < 2, new, 0.0)
        new_ref[p] = new
        low_ref[p] = new.astype(BF)


def gram_kernel(x_ref, out_ref):
    for b in range(out_ref.shape[0]):
        x = x_ref[:, b * TILE : (b + 1) * TILE]
        out_ref[b] = dot_over_rows(x, x)


def diagonal_kernel(sample_total, gram_ref, tile_ref, out_ref):
    for p in range(2):
        gram = gram_ref[p]
        high = gram.astype(BF)
        low = (gram - high.astype(F32)).astype(BF)
        tile = tile_ref[p]
        for _ in range(ITERS):
            lowered = tile.astype(BF)
            gradient = dot(high, lowered) + dot(low, lowered)
            tile = proximal(tile, gradient, gradient, eye(), sample_total)
        out_ref[p] = tile


def assemble_kernel(peer_ref, me_ref, *refs):
    pieces, (cross_ref, hub_ref) = refs[:-2], refs[-2:]
    for j, piece in enumerate(pieces):
        own = peer_ref[j] == me_ref[0]
        for p in range(2):
            tile = piece[p].astype(F32)
            cross_ref[peer_ref[j], p] = jnp.where(own, 0.0, tile)

        @pl.when(own)
        def _():
            for p in range(2):
                hub_ref[p] = piece[p].astype(F32)


def call(kernel, outs, spaces, *args):
    return pl.pallas_call(
        kernel,
        out_shape=outs,
        in_specs=list(spaces) + [VMEM] * (len(args) - len(spaces)),
        out_specs=jax.tree.map(lambda _: VMEM, outs),
        compiler_params=PARAMS,
    )(*args)


def shards(samples, diag_tiles, cross_tiles, peer_cols, pair_counts):
    genes = lax.axis_size("gene")
    s, g = lax.axis_index("sample"), lax.axis_index("gene")
    rows = samples.shape[0]
    sample_total = rows * lax.axis_size("sample")
    shape = jax.ShapeDtypeStruct

    slot = lax.broadcasted_iota(jnp.int32, (genes, 2), 1)
    own = lax.broadcasted_iota(jnp.int32, (genes, 2), 0) == g
    code = jnp.where(own, slot, jnp.where(slot < pair_counts[0][:, None], peer_cols[0], 2))
    pick = jnp.where(own, slot, peer_cols[0])
    me = jnp.reshape(g, (1,)).astype(jnp.int32)
    place = jnp.reshape(s, (1,)).astype(jnp.int32)
    z, core = s // 2, s % 2
    peers = jnp.stack([g ^ (((z - back) % 8) * 2 + (core ^ other)) for back, other in ORDER])
    peers = peers.astype(jnp.int32)
    code_of_piece = jnp.take(code, peers, axis=0)
    partner = g ^ s
    my_code = lax.dynamic_index_in_dim(code, partner, 0, keepdims=False)
    my_pick = lax.dynamic_index_in_dim(pick, partner, 0, keepdims=False)

    hubs = samples[:, : 2 * TILE]
    left, right = hubs[:, :TILE], hubs[:, TILE:]
    outgoing = jnp.concatenate(
        [jnp.where(pick[:, p, None, None] == 1, right, left) for p in range(2)], axis=2
    )
    slots = lax.all_to_all(outgoing, "gene", split_axis=0, concat_axis=0, tiled=True)

    everyone = jnp.stack(ring_gather(hubs))
    arranged = jnp.concatenate(
        [jnp.where(my_pick[p] == 1, everyone[:, :, TILE:], everyone[:, :, :TILE]) for p in range(2)],
        axis=2,
    )
    peer_rows = mirror(arranged)

    grams = call(gram_kernel, shape(diag_tiles.shape, F32), [], samples)
    my_gram = lax.psum_scatter(grams, "sample", scatter_dimension=0, tiled=True)
    my_diag = lax.dynamic_slice_in_dim(diag_tiles, 2 * s, 2, 0)
    my_diag = call(
        functools.partial(diagonal_kernel, sample_total), shape(my_diag.shape, F32), [], my_gram, my_diag
    )
    all_diag = lax.all_gather(my_diag, "sample", axis=0, tiled=True)

    tile = jnp.where(s == 0, diag_tiles[:2], lax.dynamic_index_in_dim(cross_tiles[0], partner, 0, False))
    pair = tile.shape
    pieces = None
    for iteration in range(ITERS):
        if iteration == 0:
            columns = call(
                first_columns_kernel,
                shape(hubs.shape, BF),
                [SMEM, SMEM],
                code, me, slots, cross_tiles[0], diag_tiles[:2],
            )
        else:
            columns = call(
                later_columns_kernel,
                shape(hubs.shape, BF),
                [SMEM, SMEM],
                code_of_piece, peers, slots, *pieces,
            )
        gradient = call(
            gradient_kernel, shape(pair, F32), [SMEM], my_code, peer_rows, *ring_gather(columns)
        )
        tile, lowered = call(
            functools.partial(step_kernel, sample_total),
            [shape(pair, F32), shape(pair, BF)],
            [SMEM, SMEM],
            my_code, place, tile, gradient, mirror(gradient),
        )
        pieces = ring_gather(lowered)
    cross, hub = call(
        assemble_kernel,
        [shape(cross_tiles.shape[1:], F32), shape(pair, F32)],
        [SMEM, SMEM],
        peers, me, *pieces,
    )
    return lax.dynamic_update_slice(all_diag, hub, (0, 0, 0)), cross[None]


def solution(mesh):
    in_specs = (
        P("sample", "gene"),
        P("gene", None, None),
        P("gene", None, None, None, None),
        P("gene", None, None),
        P("gene", None),
    )
    out_specs = (P("gene", None, None), P("gene", None, None, None, None))
    return jax.shard_map(shards, mesh=mesh, in_specs=in_specs, out_specs=out_specs, check_vma=False)
```

```python
import functools

import jax
import jax.numpy as jnp
from jax import lax
from jax.experimental import pallas as pl
from jax.experimental.pallas import tpu as pltpu
from jax.sharding import PartitionSpec as P

ITERS = 2
STEP = 0.5
SHRINK = 0.02
TILE = 128
BF = jnp.bfloat16
F32 = jnp.float32

BACK = (0, 1, -1, 2, -2, 3, -3, 4)
ORDER = tuple((back, other) for other in (0, 1) for back in BACK)

VMEM = pl.BlockSpec(memory_space=pltpu.VMEM)
SMEM = pl.BlockSpec(memory_space=pltpu.SMEM)
ANY = pl.BlockSpec(memory_space=pl.ANY)
PARAMS = pltpu.CompilerParams(vmem_limit_bytes=48 * 1024 * 1024)


def shift_z(x, chips):
    count = lax.axis_size("sample")
    return lax.ppermute(x, "sample", [(i, (i + 2 * chips) % count) for i in range(count)])


def swap_core(x):
    count = lax.axis_size("sample")
    return lax.ppermute(x, "sample", [(i, i ^ 1) for i in range(count)])


def gather_shards(x):
    own = [x] + [shift_z(x, back) for back in BACK[1:]]
    return own + [swap_core(piece) for piece in own]


def mirror(x):
    samples, genes = lax.axis_size("sample"), lax.axis_size("gene")
    pairs = [(s * genes + g, s * genes + (g ^ s)) for s in range(samples) for g in range(genes)]
    return lax.ppermute(x, ("sample", "gene"), pairs)


def dot(a, b):
    return jnp.dot(a, b, preferred_element_type=F32)


def dot_over_rows(a, b):
    return lax.dot_general(a, b, (((0,), (0,)), ((), ())), preferred_element_type=F32)


def column_of(cols_ref, counts_ref, h, p):
    live = jnp.where(p < counts_ref[h], cols_ref[h, p], 2)
    return jnp.where(h == lax.axis_index("gene"), p, live)


def pick_blocks(cols_ref, h, own, left, right):
    picks = [jnp.where(own, p, cols_ref[h, p]) for p in range(2)]
    return jnp.concatenate([jnp.where(pick == 1, right, left) for pick in picks], axis=-1)


def outgoing_kernel(cols_ref, x_ref, hubs_ref, out_ref):
    left, right = x_ref[:, :TILE], x_ref[:, TILE:]
    hubs_ref[...] = x_ref[...]
    for h in range(out_ref.shape[0]):
        out_ref[h] = pick_blocks(cols_ref, h, h == lax.axis_index("gene"), left, right)


def arrange_kernel(cols_ref, *refs):
    pieces, out_ref = refs[:-1], refs[-1]
    s, g = lax.axis_index("sample"), lax.axis_index("gene")
    for j, piece in enumerate(pieces):
        out_ref[j] = pick_blocks(cols_ref, g ^ s, s == 0, piece[:, :TILE], piece[:, TILE:])


def placed(tiles, columns):
    zero = jnp.zeros((TILE, TILE), BF)
    rows = [
        jnp.concatenate([jnp.where(column == c, tile.astype(BF), zero) for c in range(2)], axis=1)
        for tile, column in zip(tiles, columns)
    ]
    return jnp.concatenate(rows, axis=0)


def first_columns_kernel(cols_ref, counts_ref, slots_ref, cross_ref, hub_ref, y_ref):
    total = jnp.zeros(y_ref.shape, F32)
    for h in range(cross_ref.shape[0]):
        own = h == lax.axis_index("gene")
        tiles = [jnp.where(own, hub_ref[p], cross_ref[h, p]) for p in range(2)]
        columns = [column_of(cols_ref, counts_ref, h, p) for p in range(2)]
        total += dot(slots_ref[h], placed(tiles, columns))
    y_ref[...] = total.astype(BF)


def peer_of(j):
    back, other = ORDER[j]
    s, g = lax.axis_index("sample"), lax.axis_index("gene")
    chips = lax.axis_size("sample") // 2
    return g ^ (lax.rem(s // 2 - back + chips, chips) * 2 + (s % 2 ^ other))


def later_columns_kernel(cols_ref, counts_ref, slots_ref, *refs):
    pieces, y_ref = refs[:-1], refs[-1]
    total = jnp.zeros(y_ref.shape, F32)
    for j, piece in enumerate(pieces):
        h = peer_of(j)
        columns = [column_of(cols_ref, counts_ref, h, p) for p in range(2)]
        total += dot(slots_ref[h], placed([piece[0], piece[1]], columns))
    y_ref[...] = total.astype(BF)


def my_column(cols_ref, counts_ref, p):
    return column_of(cols_ref, counts_ref, lax.axis_index("gene") ^ lax.axis_index("sample"), p)


def gradient_kernel(cols_ref, counts_ref, rows_ref, *refs):
    pieces, out_ref = refs[:-1], refs[-1]
    total = jnp.zeros((2 * TILE, 2 * TILE), F32)
    for j, piece in enumerate(pieces):
        total += dot_over_rows(rows_ref[j], piece[...])
    for p in range(2):
        rows = total[p * TILE : (p + 1) * TILE]
        out_ref[p] = jnp.where(
            my_column(cols_ref, counts_ref, p) == 1, rows[:, TILE:], rows[:, :TILE]
        )


def proximal(tile, gradient, mirrored, diagonal, sample_total):
    symmetric = 0.5 * (gradient + mirrored.T) / sample_total
    stepped = tile - STEP * symmetric
    shrunk = jnp.where(
        stepped > 0, jnp.maximum(stepped - SHRINK, 0.0), jnp.minimum(stepped + SHRINK, 0.0)
    )
    barrier = 0.5 * (stepped + jnp.sqrt(stepped * stepped + 4.0 * STEP))
    return jnp.where(diagonal, barrier, shrunk)


def eye():
    shape = (TILE, TILE)
    return lax.broadcasted_iota(jnp.int32, shape, 0) == lax.broadcasted_iota(jnp.int32, shape, 1)


def step_kernel(
    sample_total, cols_ref, counts_ref, tile_ref, grad_ref, mirrored_ref, new_ref, low_ref
):
    is_hub = lax.axis_index("sample") == 0
    on_diagonal = jnp.where(is_hub, eye().astype(F32), 0.0) > 0.5
    for p in range(2):
        new = proximal(tile_ref[p], grad_ref[p], mirrored_ref[p], on_diagonal, sample_total)
        new = jnp.where(my_column(cols_ref, counts_ref, p) < 2, new, 0.0)
        new_ref[p] = new
        low_ref[p] = new.astype(BF)


def gram_kernel(x_ref, out_ref):
    for b in range(out_ref.shape[0]):
        x = x_ref[:, b * TILE : (b + 1) * TILE]
        out_ref[b] = dot_over_rows(x, x)


def diagonal_kernel(sample_total, gram_ref, tile_ref, after_ref, out_ref):
    for p in range(2):
        gram = gram_ref[p]
        high = gram.astype(BF)
        low = (gram - high.astype(F32)).astype(BF)
        tile = tile_ref[p]
        for _ in range(ITERS):
            lowered = tile.astype(BF)
            gradient = dot(high, lowered) + dot(low, lowered)
            tile = proximal(tile, gradient, gradient, eye(), sample_total)
        out_ref[p] = tile


def copy_kernel(x_ref, after_ref, out_ref):
    out_ref[...] = x_ref[...]


def assemble_kernel(*refs):
    pieces, (cross_ref, hub_ref) = refs[:-2], refs[-2:]
    for j, piece in enumerate(pieces):
        h = peer_of(j)
        own = h == lax.axis_index("gene")
        for p in range(2):
            cross_ref[h, p] = jnp.where(own, 0.0, piece[p].astype(F32))

        @pl.when(own)
        def _():
            for p in range(2):
                hub_ref[p] = piece[p].astype(F32)


def call(kernel, outs, spaces, *args, grid=()):
    return pl.pallas_call(
        kernel,
        grid=grid,
        out_shape=outs,
        in_specs=list(spaces) + [VMEM] * (len(args) - len(spaces)),
        out_specs=jax.tree.map(lambda _: VMEM, outs),
        compiler_params=PARAMS,
    )(*args)


def shards(samples, diag_tiles, cross_tiles, peer_cols, pair_counts):
    s, g = lax.axis_index("sample"), lax.axis_index("gene")
    genes = lax.axis_size("gene")
    rows = samples.shape[0]
    sample_total = rows * lax.axis_size("sample")
    shape = jax.ShapeDtypeStruct
    cols, counts = peer_cols[0], pair_counts[0]
    part = shape((rows, 2 * TILE), BF)
    hub_columns = pl.BlockSpec(part.shape, lambda i: (0, 0))

    hubs, outgoing = call(
        outgoing_kernel, [part, shape((genes,) + part.shape, BF)], [SMEM, hub_columns], cols, samples, grid=(1,)
    )
    slots = lax.all_to_all(outgoing, "gene", split_axis=0, concat_axis=0, tiled=True)
    peer_rows = mirror(
        call(arrange_kernel, shape((len(ORDER),) + part.shape, BF), [SMEM], cols, *gather_shards(hubs))
    )

    grams = call(gram_kernel, shape(diag_tiles.shape, F32), [], samples)
    my_gram = lax.psum_scatter(grams, "sample", scatter_dimension=0, tiled=True)

    tile = jnp.where(s == 0, diag_tiles[:2], lax.dynamic_index_in_dim(cross_tiles[0], g ^ s, 0, False))
    pair = tile.shape
    for iteration in range(ITERS):
        if iteration == 0:
            columns = call(
                first_columns_kernel, part, [SMEM, SMEM], cols, counts, slots, cross_tiles[0], diag_tiles[:2]
            )
        else:
            columns = call(later_columns_kernel, part, [SMEM, SMEM], cols, counts, slots, *pieces)
        gradient = call(
            gradient_kernel, shape(pair, F32), [SMEM, SMEM], cols, counts, peer_rows, *gather_shards(columns)
        )
        tile, lowered = call(
            functools.partial(step_kernel, sample_total),
            [shape(pair, F32), shape(pair, BF)],
            [SMEM, SMEM],
            cols, counts, tile, gradient, mirror(gradient),
        )
        pieces = gather_shards(lowered)

    my_diag = call(
        functools.partial(diagonal_kernel, sample_total),
        shape(pair, F32),
        [VMEM, VMEM, ANY],
        my_gram, lax.dynamic_slice_in_dim(diag_tiles, 2 * s, 2, 0), columns,
    )
    all_diag = lax.all_gather(my_diag, "sample", axis=0, tiled=True)
    all_diag = call(copy_kernel, shape(diag_tiles.shape, F32), [VMEM, ANY], all_diag, lowered)

    cross, hub = call(assemble_kernel, [shape(cross_tiles.shape[1:], F32), shape(pair, F32)], [], *pieces)
    return lax.dynamic_update_slice(all_diag, hub, (0, 0, 0)), cross[None]


def solution(mesh):
    in_specs = (
        P("sample", "gene"),
        P("gene", None, None),
        P("gene", None, None, None, None),
        P("gene", None, None),
        P("gene", None),
    )
    out_specs = (P("gene", None, None), P("gene", None, None, None, None))
    return jax.shard_map(shards, mesh=mesh, in_specs=in_specs, out_specs=out_specs, check_vma=False)
```

```python
import functools

import jax
import jax.numpy as jnp
from jax import lax
from jax.experimental import pallas as pl
from jax.experimental.pallas import tpu as pltpu
from jax.sharding import PartitionSpec as P

ITERS = 2
STEP = 0.5
SHRINK = 0.02
TILE = 128
BF = jnp.bfloat16
F32 = jnp.float32

ALL = (0, 1, -1, 2, -2, 3, -3, 4)
PARITY = (0, 2, -2, 4)
PARTNER = 2


def order(backs):
    return tuple((back, other) for other in (0, 1) for back in backs)


VMEM = pl.BlockSpec(memory_space=pltpu.VMEM)
SMEM = pl.BlockSpec(memory_space=pltpu.SMEM)
ANY = pl.BlockSpec(memory_space=pl.ANY)
PARAMS = pltpu.CompilerParams(vmem_limit_bytes=48 * 1024 * 1024)


def shift_z(x, chips):
    count = lax.axis_size("sample")
    return lax.ppermute(x, "sample", [(i, (i + 2 * chips) % count) for i in range(count)])


def swap_core(x):
    count = lax.axis_size("sample")
    return lax.ppermute(x, "sample", [(i, i ^ 1) for i in range(count)])


def gather_shards(x, backs):
    own = [x] + [shift_z(x, back) for back in backs[1:]]
    return own + [swap_core(piece) for piece in own]


def swap_owner(x, sample_xor, gene_xor):
    samples, genes = lax.axis_size("sample"), lax.axis_size("gene")
    pairs = [
        (s * genes + g, (s ^ sample_xor) * genes + (g ^ gene_xor(s)))
        for s in range(samples)
        for g in range(genes)
    ]
    return lax.ppermute(x, ("sample", "gene"), pairs)


def dot(a, b):
    return jnp.dot(a, b, preferred_element_type=F32)


def dot_over_rows(a, b):
    return lax.dot_general(a, b, (((0,), (0,)), ((), ())), preferred_element_type=F32)


def column_of(cols_ref, counts_ref, h, p):
    live = jnp.where(p < counts_ref[h], cols_ref[h, p], 2)
    return jnp.where(h == lax.axis_index("gene"), p, live)


def pick_blocks(cols_ref, h, own, left, right):
    picks = [jnp.where(own, p, cols_ref[h, p]) for p in range(2)]
    return jnp.concatenate([jnp.where(pick == 1, right, left) for pick in picks], axis=-1)


def outgoing_kernel(cols_ref, x_ref, hubs_ref, out_ref):
    left, right = x_ref[:, :TILE], x_ref[:, TILE:]
    hubs_ref[...] = x_ref[...]
    for h in range(out_ref.shape[0]):
        out_ref[h] = pick_blocks(cols_ref, h, h == lax.axis_index("gene"), left, right)


def arrange_kernel(cols_ref, *refs):
    pieces, outs = refs[:-2], refs[-2:]
    g = lax.axis_index("gene")
    for owner, out_ref in zip(owners(), outs):
        for j, piece in enumerate(pieces):
            out_ref[j] = pick_blocks(cols_ref, g ^ owner, owner == 0, piece[:, :TILE], piece[:, TILE:])


def owners():
    s = lax.axis_index("sample")
    return s, s ^ PARTNER


def placed(tiles, columns):
    zero = jnp.zeros((TILE, TILE), BF)
    rows = [
        jnp.concatenate([jnp.where(column == c, tile.astype(BF), zero) for c in range(2)], axis=1)
        for tile, column in zip(tiles, columns)
    ]
    return jnp.concatenate(rows, axis=0)


def first_columns_kernel(cols_ref, counts_ref, slots_ref, cross_ref, hub_ref, y_ref):
    total = jnp.zeros(y_ref.shape, F32)
    for h in range(cross_ref.shape[0]):
        own = h == lax.axis_index("gene")
        tiles = [jnp.where(own, hub_ref[p], cross_ref[h, p]) for p in range(2)]
        columns = [column_of(cols_ref, counts_ref, h, p) for p in range(2)]
        total += dot(slots_ref[h], placed(tiles, columns))
    y_ref[...] = total.astype(BF)


def peer_of(j):
    back, other = order(ALL)[j]
    s, g = lax.axis_index("sample"), lax.axis_index("gene")
    chips = lax.axis_size("sample") // 2
    return g ^ (lax.rem(s // 2 - back + chips, chips) * 2 + (s % 2 ^ other))


def later_columns_kernel(cols_ref, counts_ref, slots_ref, *refs):
    pieces, y_ref = refs[:-1], refs[-1]
    total = jnp.zeros(y_ref.shape, F32)
    for j, piece in enumerate(pieces):
        h = peer_of(j)
        columns = [column_of(cols_ref, counts_ref, h, p) for p in range(2)]
        total += dot(slots_ref[h], placed([piece[0], piece[1]], columns))
    y_ref[...] = total.astype(BF)


def gradient_kernel(cols_ref, counts_ref, own_rows_ref, partner_rows_ref, *refs):
    pieces, outs = refs[:-2], refs[-2:]
    g = lax.axis_index("gene")
    for owner, rows_ref, out_ref in zip(owners(), (own_rows_ref, partner_rows_ref), outs):
        total = jnp.zeros((2 * TILE, 2 * TILE), F32)
        for j, piece in enumerate(pieces):
            total += dot_over_rows(rows_ref[j], piece[...])
        for p in range(2):
            rows = total[p * TILE : (p + 1) * TILE]
            column = column_of(cols_ref, counts_ref, g ^ owner, p)
            out_ref[p] = jnp.where(column == 1, rows[:, TILE:], rows[:, :TILE])


def proximal(tile, gradient, mirrored, diagonal, sample_total):
    symmetric = 0.5 * (gradient + mirrored.T) / sample_total
    stepped = tile - STEP * symmetric
    shrunk = jnp.where(
        stepped > 0, jnp.maximum(stepped - SHRINK, 0.0), jnp.minimum(stepped + SHRINK, 0.0)
    )
    barrier = 0.5 * (stepped + jnp.sqrt(stepped * stepped + 4.0 * STEP))
    return jnp.where(diagonal, barrier, shrunk)


def eye():
    shape = (TILE, TILE)
    return lax.broadcasted_iota(jnp.int32, shape, 0) == lax.broadcasted_iota(jnp.int32, shape, 1)


def step_kernel(sample_total, cols_ref, counts_ref, tile_ref, *refs):
    (own_ref, partner_ref, mirrored_ref, far_ref), (new_ref, low_ref) = refs[:-2], refs[-2:]
    s, g = lax.axis_index("sample"), lax.axis_index("gene")
    on_diagonal = jnp.where(s == 0, eye().astype(F32), 0.0) > 0.5
    for p in range(2):
        gradient, mirrored = own_ref[p] + partner_ref[p], mirrored_ref[p] + far_ref[p]
        new = proximal(tile_ref[p], gradient, mirrored, on_diagonal, sample_total)
        new = jnp.where(column_of(cols_ref, counts_ref, g ^ s, p) < 2, new, 0.0)
        new_ref[p] = new
        low_ref[p] = new.astype(BF)


def upper(strict):
    shape = (TILE, TILE)
    row, column = lax.broadcasted_iota(jnp.int32, shape, 0), lax.broadcasted_iota(jnp.int32, shape, 1)
    return row < column if strict else row <= column


def gram_kernel(x_ref, after_ref, out_ref):
    for b in range(out_ref.shape[0]):
        x = x_ref[:, 2 * b * TILE : 2 * (b + 1) * TILE]
        first, second = (dot_over_rows(x[:, at : at + TILE], x[:, at : at + TILE]) for at in (0, TILE))
        out_ref[b, :TILE] = jnp.where(upper(False), first, second)
        diagonal = jnp.sum(jnp.where(eye(), second, 0.0), axis=0, keepdims=True)
        out_ref[b, TILE:] = jnp.broadcast_to(diagonal, (8, TILE))


def diagonal_kernel(sample_total, packed_ref, tile_ref, after_ref, out_ref):
    packed = packed_ref[0, :TILE]
    turned = packed.T
    first = jnp.where(upper(False), packed, turned)
    second = jnp.where(upper(True), turned, packed)
    second = jnp.where(eye(), packed_ref[0, TILE : TILE + 1], second)
    for p, gram in enumerate((first, second)):
        high = gram.astype(BF)
        low = (gram - high.astype(F32)).astype(BF)
        tile = tile_ref[p]
        for _ in range(ITERS):
            lowered = tile.astype(BF)
            gradient = dot(high, lowered) + dot(low, lowered)
            tile = proximal(tile, gradient, gradient, eye(), sample_total)
        out_ref[p] = tile.astype(BF)


def copy_kernel(x_ref, after_ref, out_ref):
    out_ref[...] = x_ref[...].astype(F32)


def assemble_kernel(*refs):
    pieces, (cross_ref, hub_ref) = refs[:-2], refs[-2:]
    for j, piece in enumerate(pieces):
        h = peer_of(j)
        own = h == lax.axis_index("gene")
        for p in range(2):
            cross_ref[h, p] = jnp.where(own, 0.0, piece[p].astype(F32))

        @pl.when(own)
        def _():
            for p in range(2):
                hub_ref[p] = piece[p].astype(F32)


def call(kernel, outs, spaces, *args, grid=()):
    return pl.pallas_call(
        kernel,
        grid=grid,
        out_shape=outs,
        in_specs=list(spaces) + [VMEM] * (len(args) - len(spaces)),
        out_specs=jax.tree.map(lambda _: VMEM, outs),
        compiler_params=PARAMS,
    )(*args)


def shards(samples, diag_tiles, cross_tiles, peer_cols, pair_counts):
    s, g = lax.axis_index("sample"), lax.axis_index("gene")
    genes = lax.axis_size("gene")
    rows = samples.shape[0]
    sample_total = rows * lax.axis_size("sample")
    shape = jax.ShapeDtypeStruct
    cols, counts = peer_cols[0], pair_counts[0]
    part = shape((rows, 2 * TILE), BF)
    hub_columns = pl.BlockSpec(part.shape, lambda i: (0, 0))

    hubs, outgoing = call(
        outgoing_kernel, [part, shape((genes,) + part.shape, BF)], [SMEM, hub_columns], cols, samples, grid=(1,)
    )
    slots = lax.all_to_all(outgoing, "gene", split_axis=0, concat_axis=0, tiled=True)
    rows_shape = shape((len(order(PARITY)),) + part.shape, BF)
    arranged = call(arrange_kernel, [rows_shape] * 2, [SMEM], cols, *gather_shards(hubs, PARITY))
    own_rows = swap_owner(arranged[0], 0, lambda s: s)
    partner_rows = swap_owner(arranged[1], 0, lambda s: s ^ PARTNER)

    packed = shape((diag_tiles.shape[0] // 2, TILE + 8, TILE), F32)
    grams = call(gram_kernel, packed, [VMEM, ANY], samples, outgoing)
    my_gram = lax.psum_scatter(grams, "sample", scatter_dimension=0, tiled=True)

    tile = jnp.where(s == 0, diag_tiles[:2], lax.dynamic_index_in_dim(cross_tiles[0], g ^ s, 0, False))
    pair = tile.shape
    for iteration in range(ITERS):
        if iteration == 0:
            columns = call(
                first_columns_kernel, part, [SMEM, SMEM], cols, counts, slots, cross_tiles[0], diag_tiles[:2]
            )
        else:
            columns = call(later_columns_kernel, part, [SMEM, SMEM], cols, counts, slots, *pieces)
        own, partner = call(
            gradient_kernel,
            [shape(pair, F32)] * 2,
            [SMEM, SMEM],
            cols, counts, own_rows, partner_rows, *gather_shards(columns, PARITY),
        )
        others = (
            swap_owner(partner, PARTNER, lambda s: 0),
            swap_owner(own, 0, lambda s: s),
            swap_owner(partner, PARTNER, lambda s: s ^ PARTNER),
        )
        tile, lowered = call(
            functools.partial(step_kernel, sample_total),
            [shape(pair, F32), shape(pair, BF)],
            [SMEM, SMEM],
            cols, counts, tile, own, *others,
        )
        pieces = gather_shards(lowered, ALL)

    my_diag = call(
        functools.partial(diagonal_kernel, sample_total),
        shape(pair, BF),
        [VMEM, VMEM, ANY],
        my_gram, lax.dynamic_slice_in_dim(diag_tiles, 2 * s, 2, 0), columns,
    )
    all_diag = lax.all_gather(my_diag, "sample", axis=0, tiled=True)
    all_diag = call(copy_kernel, shape(diag_tiles.shape, F32), [VMEM, ANY], all_diag, lowered)

    cross, hub = call(assemble_kernel, [shape(cross_tiles.shape[1:], F32), shape(pair, F32)], [], *pieces)
    return lax.dynamic_update_slice(all_diag, hub, (0, 0, 0)), cross[None]


def solution(mesh):
    in_specs = (
        P("sample", "gene"),
        P("gene", None, None),
        P("gene", None, None, None, None),
        P("gene", None, None),
        P("gene", None),
    )
    out_specs = (P("gene", None, None), P("gene", None, None, None, None))
    return jax.shard_map(shards, mesh=mesh, in_specs=in_specs, out_specs=out_specs, check_vma=False)
```

```python
import functools

import jax
import jax.numpy as jnp
from jax import lax
from jax.experimental import pallas as pl
from jax.experimental.pallas import tpu as pltpu
from jax.sharding import PartitionSpec as P

ITERS = 2
STEP = 0.5
SHRINK = 0.02
TILE = 128
BF = jnp.bfloat16
F32 = jnp.float32

ALL = (0, 1, -1, 2, -2, 3, -3, 4)
PARITY = (0, 2, -2, 4)
MASKS = tuple(
    4 * y + x
    for (x, y) in (
        (0, 0), (2, 2), (2, 0), (0, 2), (2, 1), (0, 3), (2, 3), (0, 1),
        (1, 0), (3, 2), (3, 0), (1, 2), (1, 1), (3, 3), (1, 3), (3, 1),
    )
)
PARTNER = 2


def order(backs):
    return tuple((back, other) for other in (0, 1) for back in backs)


VMEM = pl.BlockSpec(memory_space=pltpu.VMEM)
SMEM = pl.BlockSpec(memory_space=pltpu.SMEM)
ANY = pl.BlockSpec(memory_space=pl.ANY)
PARAMS = pltpu.CompilerParams(vmem_limit_bytes=48 * 1024 * 1024)


def shift_z(x, chips):
    count = lax.axis_size("sample")
    return lax.ppermute(x, "sample", [(i, (i + 2 * chips) % count) for i in range(count)])


def swap_core(x):
    count = lax.axis_size("sample")
    return lax.ppermute(x, "sample", [(i, i ^ 1) for i in range(count)])


def gather_shards(x, backs):
    own = [x] + [shift_z(x, back) for back in backs[1:]]
    return own + [swap_core(piece) for piece in own]


def swap_owner(x, sample_xor, gene_xor):
    samples, genes = lax.axis_size("sample"), lax.axis_size("gene")
    pairs = [
        (s * genes + g, (s ^ sample_xor) * genes + (g ^ gene_xor(s)))
        for s in range(samples)
        for g in range(genes)
    ]
    return lax.ppermute(x, ("sample", "gene"), pairs)


def dot(a, b):
    return jnp.dot(a, b, preferred_element_type=F32)


def dot_over_rows(a, b):
    return lax.dot_general(a, b, (((0,), (0,)), ((), ())), preferred_element_type=F32)


def column_of(cols_ref, counts_ref, h, p):
    live = jnp.where(p < counts_ref[h], cols_ref[h, p], 2)
    return jnp.where(h == lax.axis_index("gene"), p, live)


def pick_blocks(cols_ref, h, own, left, right):
    picks = [jnp.where(own, p, cols_ref[h, p]) for p in range(2)]
    return jnp.concatenate([jnp.where(pick == 1, right, left) for pick in picks], axis=-1)


def outgoing_kernel(cols_ref, x_ref, out_ref):
    left, right = x_ref[:, :TILE], x_ref[:, TILE:]
    for h in range(out_ref.shape[0]):
        out_ref[h] = pick_blocks(cols_ref, h, h == lax.axis_index("gene"), left, right)


def arrange_kernel(cols_ref, *refs):
    pieces, outs = refs[:-2], refs[-2:]
    g = lax.axis_index("gene")
    for owner, out_ref in zip(owners(), outs):
        for j, piece in enumerate(pieces):
            out_ref[j] = pick_blocks(cols_ref, g ^ mask_of(owner), owner == 0, piece[:, :TILE], piece[:, TILE:])


def mask_of(s):
    mask = s * 0
    for at, value in enumerate(MASKS):
        mask = jnp.where(s == at, value, mask)
    return mask


def owners():
    s = lax.axis_index("sample")
    return s, s ^ PARTNER


def placed(tiles, columns):
    zero = jnp.zeros((TILE, TILE), BF)
    rows = [
        jnp.concatenate([jnp.where(column == c, tile.astype(BF), zero) for c in range(2)], axis=1)
        for tile, column in zip(tiles, columns)
    ]
    return jnp.concatenate(rows, axis=0)


def first_columns_kernel(cols_ref, counts_ref, slots_ref, cross_ref, hub_ref, y_ref):
    total = jnp.zeros(y_ref.shape, F32)
    for h in range(cross_ref.shape[0]):
        own = h == lax.axis_index("gene")
        tiles = [jnp.where(own, hub_ref[p], cross_ref[h, p]) for p in range(2)]
        columns = [column_of(cols_ref, counts_ref, h, p) for p in range(2)]
        total += dot(slots_ref[h], placed(tiles, columns))
    y_ref[...] = total.astype(BF)


def peer_of(j):
    back, other = order(ALL)[j]
    s, g = lax.axis_index("sample"), lax.axis_index("gene")
    chips = lax.axis_size("sample") // 2
    return g ^ mask_of(lax.rem(s // 2 - back + chips, chips) * 2 + (s % 2 ^ other))


def later_columns_kernel(cols_ref, counts_ref, slots_ref, *refs):
    pieces, y_ref = refs[:-1], refs[-1]
    total = jnp.zeros(y_ref.shape, F32)
    for j, piece in enumerate(pieces):
        h = peer_of(j)
        columns = [column_of(cols_ref, counts_ref, h, p) for p in range(2)]
        total += dot(slots_ref[h], placed([piece[0], piece[1]], columns))
    y_ref[...] = total.astype(BF)


def gradient_kernel(cols_ref, counts_ref, own_rows_ref, partner_rows_ref, *refs):
    pieces, outs = refs[:-2], refs[-2:]
    g = lax.axis_index("gene")
    for owner, rows_ref, out_ref in zip(owners(), (own_rows_ref, partner_rows_ref), outs):
        total = jnp.zeros((2 * TILE, 2 * TILE), F32)
        for j, piece in enumerate(pieces):
            total += dot_over_rows(rows_ref[j], piece[...])
        for p in range(2):
            rows = total[p * TILE : (p + 1) * TILE]
            column = column_of(cols_ref, counts_ref, g ^ mask_of(owner), p)
            out_ref[p] = jnp.where(column == 1, rows[:, TILE:], rows[:, :TILE])


def proximal(tile, gradient, mirrored, diagonal, sample_total):
    symmetric = 0.5 * (gradient + mirrored.T) / sample_total
    stepped = tile - STEP * symmetric
    shrunk = jnp.where(
        stepped > 0, jnp.maximum(stepped - SHRINK, 0.0), jnp.minimum(stepped + SHRINK, 0.0)
    )
    barrier = 0.5 * (stepped + jnp.sqrt(stepped * stepped + 4.0 * STEP))
    return jnp.where(diagonal, barrier, shrunk)


def eye():
    shape = (TILE, TILE)
    return lax.broadcasted_iota(jnp.int32, shape, 0) == lax.broadcasted_iota(jnp.int32, shape, 1)


def step_kernel(sample_total, cols_ref, counts_ref, tile_ref, *refs):
    (own_ref, partner_ref, mirrored_ref, far_ref), (new_ref, low_ref) = refs[:-2], refs[-2:]
    s, g = lax.axis_index("sample"), lax.axis_index("gene")
    on_diagonal = jnp.where(s == 0, eye().astype(F32), 0.0) > 0.5
    for p in range(2):
        gradient, mirrored = own_ref[p] + partner_ref[p], mirrored_ref[p] + far_ref[p]
        new = proximal(tile_ref[p], gradient, mirrored, on_diagonal, sample_total)
        new = jnp.where(column_of(cols_ref, counts_ref, g ^ mask_of(s), p) < 2, new, 0.0)
        new_ref[p] = new
        low_ref[p] = new.astype(BF)


def upper(strict):
    shape = (TILE, TILE)
    row, column = lax.broadcasted_iota(jnp.int32, shape, 0), lax.broadcasted_iota(jnp.int32, shape, 1)
    return row < column if strict else row <= column


def gram_kernel(x_ref, after_ref, out_ref):
    for b in range(out_ref.shape[0]):
        x = x_ref[:, 2 * b * TILE : 2 * (b + 1) * TILE]
        first, second = (dot_over_rows(x[:, at : at + TILE], x[:, at : at + TILE]) for at in (0, TILE))
        out_ref[b, :TILE] = jnp.where(upper(False), first, second)
        diagonal = jnp.sum(jnp.where(eye(), second, 0.0), axis=0, keepdims=True)
        out_ref[b, TILE:] = jnp.broadcast_to(diagonal, (8, TILE))


def diagonal_kernel(sample_total, packed_ref, tile_ref, after_ref, out_ref):
    packed = packed_ref[0, :TILE]
    turned = packed.T
    first = jnp.where(upper(False), packed, turned)
    second = jnp.where(upper(True), turned, packed)
    second = jnp.where(eye(), packed_ref[0, TILE : TILE + 1], second)
    for p, gram in enumerate((first, second)):
        high = gram.astype(BF)
        low = (gram - high.astype(F32)).astype(BF)
        tile = tile_ref[p]
        for _ in range(ITERS):
            lowered = tile.astype(BF)
            gradient = dot(high, lowered) + dot(low, lowered)
            tile = proximal(tile, gradient, gradient, eye(), sample_total)
        lowered = tile.astype(BF)
        rest = jnp.sum(jnp.where(eye(), tile - lowered.astype(F32), 0.0), axis=0, keepdims=True)
        out_ref[p, :TILE] = lowered
        out_ref[p, TILE:] = jnp.broadcast_to(rest, (16, TILE)).astype(BF)


def widen_kernel(x_ref, after_ref, out_ref):
    for b in range(out_ref.shape[0]):
        rest = x_ref[b, TILE:].astype(F32)[:1]
        out_ref[b] = x_ref[b, :TILE].astype(F32) + jnp.where(eye(), rest, 0.0)


def assemble_kernel(*refs):
    pieces, (diag_in_ref, cross_ref, diag_ref, hub_ref, sem) = refs[:-5], refs[-5:]
    for j, piece in enumerate(pieces):
        h = peer_of(j)
        own = h == lax.axis_index("gene")
        for p in range(2):
            cross_ref[h, p] = jnp.where(own, 0.0, piece[p].astype(F32))

        @pl.when(own)
        def _():
            for p in range(2):
                hub_ref[p] = piece[p].astype(F32)

    copy = pltpu.make_async_copy(hub_ref, diag_ref.at[pl.ds(0, 2)], sem)
    copy.start()
    copy.wait()


def call(kernel, outs, spaces, *args):
    return pl.pallas_call(
        kernel,
        out_shape=outs,
        in_specs=list(spaces) + [VMEM] * (len(args) - len(spaces)),
        out_specs=jax.tree.map(lambda _: VMEM, outs),
        compiler_params=PARAMS,
    )(*args)


def shards(samples, diag_tiles, cross_tiles, peer_cols, pair_counts):
    s, g = lax.axis_index("sample"), lax.axis_index("gene")
    genes = lax.axis_size("gene")
    rows = samples.shape[0]
    sample_total = rows * lax.axis_size("sample")
    shape = jax.ShapeDtypeStruct
    cols, counts = peer_cols[0], pair_counts[0]
    part = shape((rows, 2 * TILE), BF)

    hubs = samples[:, : 2 * TILE]
    outgoing = call(outgoing_kernel, shape((genes,) + part.shape, BF), [SMEM], cols, hubs)
    slots = lax.all_to_all(outgoing, "gene", split_axis=0, concat_axis=0, tiled=True)
    rows_shape = shape((len(order(PARITY)),) + part.shape, BF)
    arranged = call(arrange_kernel, [rows_shape] * 2, [SMEM], cols, *gather_shards(hubs, PARITY))
    own_rows = swap_owner(arranged[0], 0, lambda s: MASKS[s])
    partner_rows = swap_owner(arranged[1], 0, lambda s: MASKS[s ^ PARTNER])

    packed = shape((diag_tiles.shape[0] // 2, TILE + 8, TILE), F32)
    grams = call(gram_kernel, packed, [VMEM, ANY], samples, outgoing)
    my_gram = lax.psum_scatter(grams, "sample", scatter_dimension=0, tiled=True)

    tile = jnp.where(s == 0, diag_tiles[:2], lax.dynamic_index_in_dim(cross_tiles[0], g ^ mask_of(s), 0, False))
    pair = tile.shape
    for iteration in range(ITERS):
        if iteration == 0:
            columns = call(
                first_columns_kernel, part, [SMEM, SMEM], cols, counts, slots, cross_tiles[0], diag_tiles[:2]
            )
        else:
            columns = call(later_columns_kernel, part, [SMEM, SMEM], cols, counts, slots, *pieces)
        own, partner = call(
            gradient_kernel,
            [shape(pair, F32)] * 2,
            [SMEM, SMEM],
            cols, counts, own_rows, partner_rows, *gather_shards(columns, PARITY),
        )
        others = (
            swap_owner(partner, PARTNER, lambda s: 0),
            swap_owner(own, 0, lambda s: MASKS[s]),
            swap_owner(partner, PARTNER, lambda s: MASKS[s ^ PARTNER]),
        )
        tile, lowered = call(
            functools.partial(step_kernel, sample_total),
            [shape(pair, F32), shape(pair, BF)],
            [SMEM, SMEM],
            cols, counts, tile, own, *others,
        )
        pieces = gather_shards(lowered, ALL)

    my_diag = call(
        functools.partial(diagonal_kernel, sample_total),
        shape((2, TILE + 16, TILE), BF),
        [VMEM, VMEM, ANY],
        my_gram, lax.dynamic_slice_in_dim(diag_tiles, 2 * s, 2, 0), columns,
    )
    all_diag = lax.all_gather(my_diag, "sample", axis=0, tiled=True)
    all_diag = call(widen_kernel, shape(diag_tiles.shape, F32), [VMEM, ANY], all_diag, lowered)

    cross, diag = pl.pallas_call(
        assemble_kernel,
        out_shape=[shape(cross_tiles.shape[1:], F32), shape(diag_tiles.shape, F32)],
        in_specs=[VMEM] * len(pieces) + [ANY],
        out_specs=[VMEM, ANY],
        scratch_shapes=[pltpu.VMEM(pair, F32), pltpu.SemaphoreType.DMA(())],
        input_output_aliases={len(pieces): 1},
        compiler_params=PARAMS,
    )(*pieces, all_diag)
    return diag, cross[None]


def solution(mesh):
    in_specs = (
        P("sample", "gene"),
        P("gene", None, None),
        P("gene", None, None, None, None),
        P("gene", None, None),
        P("gene", None),
    )
    out_specs = (P("gene", None, None), P("gene", None, None, None, None))
    return jax.shard_map(shards, mesh=mesh, in_specs=in_specs, out_specs=out_specs, check_vma=False)
```

```python
import functools

import jax
import jax.numpy as jnp
from jax import lax
from jax.experimental import pallas as pl
from jax.experimental.pallas import tpu as pltpu
from jax.sharding import PartitionSpec as P

ITERS = 2
STEP = 0.5
SHRINK = 0.02
TILE = 128
EXTRA = 16
BF = jnp.bfloat16
F32 = jnp.float32

ALL = (0, 1, -1, 2, -2, 3, -3, 4)
PARITY = (0, 2, -2, 4)
MASKS = tuple(
    4 * y + x
    for (x, y) in (
        (0, 0), (2, 2), (2, 0), (0, 2), (2, 1), (0, 3), (2, 3), (0, 1),
        (1, 0), (3, 2), (3, 0), (1, 2), (1, 1), (3, 3), (1, 3), (3, 1),
    )
)
PARTNER = 2


def order(backs):
    return tuple((back, other) for other in (0, 1) for back in backs)


VMEM = pl.BlockSpec(memory_space=pltpu.VMEM)
SMEM = pl.BlockSpec(memory_space=pltpu.SMEM)
ANY = pl.BlockSpec(memory_space=pl.ANY)
PARAMS = pltpu.CompilerParams(vmem_limit_bytes=48 * 1024 * 1024)


def shift_z(x, chips):
    count = lax.axis_size("sample")
    return lax.ppermute(x, "sample", [(i, (i + 2 * chips) % count) for i in range(count)])


def swap_core(x):
    count = lax.axis_size("sample")
    return lax.ppermute(x, "sample", [(i, i ^ 1) for i in range(count)])


def gather_shards(x, backs):
    own = [x] + [shift_z(x, back) for back in backs[1:]]
    return own + [swap_core(piece) for piece in own]


def forward_shards(x):
    up, down, up2, down2 = (shift_z(x, back) for back in (1, -1, 2, -2))
    half = x.shape[0] // 2
    far = jnp.concatenate([shift_z(up2[:half], 2), shift_z(down2[half:], -2)], axis=0)
    own = [x, up, down, up2, down2, shift_z(up2, 1), shift_z(down2, -1), far]
    return own + [swap_core(piece) for piece in own]


def swap_owner(x, sample_xor, gene_xor):
    samples, genes = lax.axis_size("sample"), lax.axis_size("gene")
    pairs = [
        (s * genes + g, (s ^ sample_xor) * genes + (g ^ gene_xor(s)))
        for s in range(samples)
        for g in range(genes)
    ]
    return lax.ppermute(x, ("sample", "gene"), pairs)


def dot(a, b):
    return jnp.dot(a, b, preferred_element_type=F32)


def dot_over_rows(a, b):
    return lax.dot_general(a, b, (((0,), (0,)), ((), ())), preferred_element_type=F32)


def column_of(cols_ref, counts_ref, h, p):
    live = jnp.where(p < counts_ref[h], cols_ref[h, p], 2)
    return jnp.where(h == lax.axis_index("gene"), p, live)


def pick_blocks(cols_ref, h, own, left, right):
    picks = [jnp.where(own, p, cols_ref[h, p]) for p in range(2)]
    return jnp.concatenate([jnp.where(pick == 1, right, left) for pick in picks], axis=-1)


def outgoing_kernel(cols_ref, x_ref, out_ref):
    left, right = x_ref[:, :TILE], x_ref[:, TILE:]
    for h in range(out_ref.shape[0]):
        out_ref[h] = pick_blocks(cols_ref, h, h == lax.axis_index("gene"), left, right)


def arrange_kernel(cols_ref, *refs):
    pieces, outs = refs[:-2], refs[-2:]
    g = lax.axis_index("gene")
    for owner, out_ref in zip(owners(), outs):
        for j, piece in enumerate(pieces):
            out_ref[j] = pick_blocks(cols_ref, g ^ mask_of(owner), owner == 0, piece[:, :TILE], piece[:, TILE:])


def mask_of(s):
    mask = s * 0
    for at, value in enumerate(MASKS):
        mask = jnp.where(s == at, value, mask)
    return mask


def owners():
    s = lax.axis_index("sample")
    return s, s ^ PARTNER


def placed(tiles, columns):
    zero = jnp.zeros((TILE, TILE), BF)
    rows = [
        jnp.concatenate([jnp.where(column == c, tile.astype(BF), zero) for c in range(2)], axis=1)
        for tile, column in zip(tiles, columns)
    ]
    return jnp.concatenate(rows, axis=0)


def first_columns_kernel(cols_ref, counts_ref, slots_ref, cross_ref, hub_ref, y_ref, tile_ref):
    s, g = lax.axis_index("sample"), lax.axis_index("gene")
    for p in range(2):
        tile_ref[p] = jnp.where(s == 0, hub_ref[p], cross_ref[g ^ mask_of(s), p])
    total = jnp.zeros(y_ref.shape, F32)
    for h in range(cross_ref.shape[0]):
        tiles = [jnp.where(h == g, hub_ref[p], cross_ref[h, p]) for p in range(2)]
        columns = [column_of(cols_ref, counts_ref, h, p) for p in range(2)]
        total += dot(slots_ref[h], placed(tiles, columns))
    y_ref[...] = total.astype(BF)


def position_of(j):
    back, other = order(ALL)[j]
    s = lax.axis_index("sample")
    chips = lax.axis_size("sample") // 2
    return lax.rem(s // 2 - back + chips, chips) * 2 + (s % 2 ^ other)


def peer_of(j):
    return lax.axis_index("gene") ^ mask_of(position_of(j))


def later_columns_kernel(cols_ref, counts_ref, slots_ref, *refs):
    pieces, y_ref = refs[:-1], refs[-1]
    total = jnp.zeros(y_ref.shape, F32)
    for j, piece in enumerate(pieces):
        h = peer_of(j)
        columns = [column_of(cols_ref, counts_ref, h, p) for p in range(2)]
        total += dot(slots_ref[h], placed([piece[p, :TILE] for p in range(2)], columns))
    y_ref[...] = total.astype(BF)


def gradient_kernel(cols_ref, counts_ref, own_rows_ref, partner_rows_ref, *refs):
    pieces, outs = refs[:-2], refs[-2:]
    g = lax.axis_index("gene")
    for owner, rows_ref, out_ref in zip(owners(), (own_rows_ref, partner_rows_ref), outs):
        total = jnp.zeros((2 * TILE, 2 * TILE), F32)
        for j, piece in enumerate(pieces):
            total += dot_over_rows(rows_ref[j], piece[...])
        for p in range(2):
            rows = total[p * TILE : (p + 1) * TILE]
            column = column_of(cols_ref, counts_ref, g ^ mask_of(owner), p)
            out_ref[p] = jnp.where(column == 1, rows[:, TILE:], rows[:, :TILE])


def proximal(tile, gradient, mirrored, diagonal, sample_total):
    symmetric = 0.5 * (gradient + mirrored.T) / sample_total
    stepped = tile - STEP * symmetric
    shrunk = jnp.where(
        stepped > 0, jnp.maximum(stepped - SHRINK, 0.0), jnp.minimum(stepped + SHRINK, 0.0)
    )
    barrier = 0.5 * (stepped + jnp.sqrt(stepped * stepped + 4.0 * STEP))
    return jnp.where(diagonal, barrier, shrunk)


def eye():
    shape = (TILE, TILE)
    return lax.broadcasted_iota(jnp.int32, shape, 0) == lax.broadcasted_iota(jnp.int32, shape, 1)


def step_kernel(sample_total, cols_ref, counts_ref, tile_ref, *refs):
    (own_ref, partner_ref, mirrored_ref, far_ref), riders = refs[:4], refs[4:-2]
    new_ref, low_ref = refs[-2:]
    s, g = lax.axis_index("sample"), lax.axis_index("gene")
    on_diagonal = jnp.where(s == 0, eye().astype(F32), 0.0) > 0.5
    for p in range(2):
        gradient, mirrored = own_ref[p] + partner_ref[p], mirrored_ref[p] + far_ref[p]
        new = proximal(tile_ref[p], gradient, mirrored, on_diagonal, sample_total)
        new = jnp.where(column_of(cols_ref, counts_ref, g ^ mask_of(s), p) < 2, new, 0.0)
        new_ref[p] = new
        low_ref[p, :TILE] = new.astype(BF)
        for rider in riders:
            low_ref[p, TILE:] = rider[p]


def upper(strict):
    shape = (TILE, TILE)
    row, column = lax.broadcasted_iota(jnp.int32, shape, 0), lax.broadcasted_iota(jnp.int32, shape, 1)
    return row < column if strict else row <= column


def gram_kernel(x_ref, after_ref, out_ref):
    for b in range(out_ref.shape[0]):
        x = x_ref[:, 2 * b * TILE : 2 * (b + 1) * TILE]
        first, second = (dot_over_rows(x[:, at : at + TILE], x[:, at : at + TILE]) for at in (0, TILE))
        out_ref[b, :TILE] = jnp.where(upper(False), first, second).astype(BF)
        diagonal = jnp.sum(jnp.where(eye(), second, 0.0), axis=0, keepdims=True)
        out_ref[b, TILE:] = jnp.broadcast_to(diagonal, (EXTRA, TILE)).astype(BF)


def diagonal_kernel(sample_total, packed_ref, tile_ref, out_ref):
    whole = sum(packed_ref[t].astype(F32) for t in range(packed_ref.shape[0]))
    packed = whole[:TILE]
    turned = packed.T
    first = jnp.where(upper(False), packed, turned)
    second = jnp.where(upper(True), turned, packed)
    second = jnp.where(eye(), whole[TILE : TILE + 1], second)
    for p, gram in enumerate((first, second)):
        high = gram.astype(BF)
        low = (gram - high.astype(F32)).astype(BF)
        tile = tile_ref[p]
        for _ in range(ITERS):
            lowered = tile.astype(BF)
            gradient = dot(high, lowered) + dot(low, lowered)
            tile = proximal(tile, gradient, gradient, eye(), sample_total)
        lowered = tile.astype(BF)
        rest = jnp.sum(jnp.where(eye(), tile - lowered.astype(F32), 0.0), axis=0, keepdims=True)
        out_ref[p, :TILE] = lowered
        out_ref[p, TILE:] = jnp.broadcast_to(rest, (EXTRA, TILE)).astype(BF)


def widen_kernel(*refs):
    pieces, out_ref = refs[:-1], refs[-1]
    for j, piece in enumerate(pieces):
        first = 2 * position_of(j)
        for p in range(2):
            rest = piece[p, 2 * TILE :].astype(F32)[:1]
            tile = piece[p, TILE : 2 * TILE].astype(F32)
            out_ref[first + p] = tile + jnp.where(eye(), rest, 0.0)


def assemble_kernel(*refs):
    pieces, (diag_in_ref, cross_ref, diag_ref, hub_ref, sem) = refs[:-5], refs[-5:]
    for j, piece in enumerate(pieces):
        h = peer_of(j)
        own = h == lax.axis_index("gene")
        for p in range(2):
            cross_ref[h, p] = jnp.where(own, 0.0, piece[p].astype(F32))

        @pl.when(own)
        def _():
            for p in range(2):
                hub_ref[p] = piece[p].astype(F32)

    copy = pltpu.make_async_copy(hub_ref, diag_ref.at[pl.ds(0, 2)], sem)
    copy.start()
    copy.wait()


def call(kernel, outs, spaces, *args, flops=10**8):
    moved = sum(x.size * x.dtype.itemsize for x in list(args) + jax.tree.leaves(outs))
    return pl.pallas_call(
        kernel,
        out_shape=outs,
        in_specs=list(spaces) + [VMEM] * (len(args) - len(spaces)),
        out_specs=jax.tree.map(lambda _: VMEM, outs),
        compiler_params=PARAMS,
        cost_estimate=pl.CostEstimate(flops=flops, bytes_accessed=moved, transcendentals=0),
    )(*args)


def shards(samples, diag_tiles, cross_tiles, peer_cols, pair_counts):
    s, g = lax.axis_index("sample"), lax.axis_index("gene")
    genes = lax.axis_size("gene")
    rows = samples.shape[0]
    sample_total = rows * lax.axis_size("sample")
    shape = jax.ShapeDtypeStruct
    cols, counts = peer_cols[0], pair_counts[0]
    part = shape((rows, 2 * TILE), BF)

    hubs = samples[:, : 2 * TILE]
    outgoing = call(outgoing_kernel, shape((genes,) + part.shape, BF), [SMEM], cols, hubs)
    slots = lax.all_to_all(outgoing, "gene", split_axis=0, concat_axis=0, tiled=True)
    rows_shape = shape((len(order(PARITY)),) + part.shape, BF)
    arranged = call(arrange_kernel, [rows_shape] * 2, [SMEM], cols, *gather_shards(hubs, PARITY))
    own_rows = swap_owner(arranged[0], 0, lambda s: MASKS[s])
    partner_rows = swap_owner(arranged[1], 0, lambda s: MASKS[s ^ PARTNER])

    packed = shape((diag_tiles.shape[0] // 2, TILE + EXTRA, TILE), BF)
    grams = call(gram_kernel, packed, [VMEM, ANY], samples, outgoing)
    my_diag = call(
        functools.partial(diagonal_kernel, sample_total),
        shape((2, TILE + EXTRA, TILE), BF),
        [],
        lax.all_to_all(grams, "sample", split_axis=0, concat_axis=0, tiled=True),
        lax.dynamic_slice_in_dim(diag_tiles, 2 * s, 2, 0),
    )

    pair = (2, TILE, TILE)
    for iteration in range(ITERS):
        if iteration == 0:
            columns, tile = call(
                first_columns_kernel, [part, shape(pair, F32)], [SMEM, SMEM], cols, counts, slots, cross_tiles[0], diag_tiles[:2]
            )
        else:
            columns = call(later_columns_kernel, part, [SMEM, SMEM], cols, counts, slots, *pieces)
        own, partner = call(
            gradient_kernel,
            [shape(pair, F32)] * 2,
            [SMEM, SMEM],
            cols, counts, own_rows, partner_rows, *gather_shards(columns, PARITY),
        )
        others = (
            swap_owner(partner, PARTNER, lambda s: 0),
            swap_owner(own, 0, lambda s: MASKS[s]),
            swap_owner(partner, PARTNER, lambda s: MASKS[s ^ PARTNER]),
        )
        riders = [my_diag] if iteration == 0 else []
        tile, lowered = call(
            functools.partial(step_kernel, sample_total),
            [shape(pair, F32), shape((2, TILE + sum(r.shape[1] for r in riders), TILE), BF)],
            [SMEM, SMEM],
            cols, counts, tile, own, *others, *riders,
        )
        if iteration == 0:
            pieces = forward_shards(lowered)
            all_diag = call(widen_kernel, shape(diag_tiles.shape, F32), [], *pieces)
        else:
            pieces = gather_shards(lowered, ALL)

    cross, diag = pl.pallas_call(
        assemble_kernel,
        out_shape=[shape(cross_tiles.shape[1:], F32), shape(diag_tiles.shape, F32)],
        in_specs=[VMEM] * len(pieces) + [ANY],
        out_specs=[VMEM, ANY],
        scratch_shapes=[pltpu.VMEM(pair, F32), pltpu.SemaphoreType.DMA(())],
        input_output_aliases={len(pieces): 1},
        compiler_params=PARAMS,
    )(*pieces, all_diag)
    return diag, cross[None]


def solution(mesh):
    in_specs = (
        P("sample", "gene"),
        P("gene", None, None),
        P("gene", None, None, None, None),
        P("gene", None, None),
        P("gene", None),
    )
    out_specs = (P("gene", None, None), P("gene", None, None, None, None))
    return jax.shard_map(shards, mesh=mesh, in_specs=in_specs, out_specs=out_specs, check_vma=False)
```

```python
import functools

import jax
import jax.numpy as jnp
from jax import lax
from jax.experimental import pallas as pl
from jax.experimental.pallas import tpu as pltpu
from jax.sharding import PartitionSpec as P

ITERS = 2
STEP = 0.5
SHRINK = 0.02
TILE = 128
EXTRA = 16
BF = jnp.bfloat16
F32 = jnp.float32

ALL = (0, 1, -1, 2, -2, 3, -3, 4)
PARITY = (0, 2, -2, 4)
MASKS = tuple(
    4 * y + x
    for (x, y) in (
        (0, 0), (2, 2), (2, 0), (0, 2), (2, 1), (0, 3), (2, 3), (0, 1),
        (1, 0), (3, 2), (3, 0), (1, 2), (1, 1), (3, 3), (1, 3), (3, 1),
    )
)
PARTNER = 2


def order(backs):
    return tuple((back, other) for other in (0, 1) for back in backs)


VMEM = pl.BlockSpec(memory_space=pltpu.VMEM)
SMEM = pl.BlockSpec(memory_space=pltpu.SMEM)
ANY = pl.BlockSpec(memory_space=pl.ANY)
PARAMS = pltpu.CompilerParams(vmem_limit_bytes=48 * 1024 * 1024)


def shift_z(x, chips):
    count = lax.axis_size("sample")
    return lax.ppermute(x, "sample", [(i, (i + 2 * chips) % count) for i in range(count)])


def swap_core(x):
    count = lax.axis_size("sample")
    return lax.ppermute(x, "sample", [(i, i ^ 1) for i in range(count)])


def gather_shards(x, backs):
    own = [x] + [shift_z(x, back) for back in backs[1:]]
    return own + [swap_core(piece) for piece in own]


def forward_shards(x):
    up, down, up2, down2 = (shift_z(x, back) for back in (1, -1, 2, -2))
    half = x.shape[0] // 2
    far = jnp.concatenate([shift_z(up2[:half], 2), shift_z(down2[half:], -2)], axis=0)
    own = [x, up, down, up2, down2, shift_z(up2, 1), shift_z(down2, -1), far]
    return own + [swap_core(piece) for piece in own]


def swap_owner(x, sample_xor, gene_xor):
    samples, genes = lax.axis_size("sample"), lax.axis_size("gene")
    pairs = [
        (s * genes + g, (s ^ sample_xor) * genes + (g ^ gene_xor(s)))
        for s in range(samples)
        for g in range(genes)
    ]
    return lax.ppermute(x, ("sample", "gene"), pairs)


def dot(a, b):
    return jnp.dot(a, b, preferred_element_type=F32)


def dot_over_rows(a, b):
    return lax.dot_general(a, b, (((0,), (0,)), ((), ())), preferred_element_type=F32)


def column_of(cols_ref, counts_ref, h, p):
    live = jnp.where(p < counts_ref[0, h], cols_ref[0, h, p], 2)
    return jnp.where(h == lax.axis_index("gene"), p, live)


def pick_blocks(cols_ref, h, own, left, right):
    picks = [jnp.where(own, p, cols_ref[0, h, p]) for p in range(2)]
    return jnp.concatenate([jnp.where(pick == 1, right, left) for pick in picks], axis=-1)


def outgoing_kernel(cols_ref, *refs):
    x_ref, out_ref = refs[-2:]
    left, right = x_ref[:, :TILE], x_ref[:, TILE:]
    for h in range(out_ref.shape[0]):
        out_ref[h] = pick_blocks(cols_ref, h, h == lax.axis_index("gene"), left, right)


def arrange_kernel(cols_ref, *refs):
    pieces, outs = refs[:-2], refs[-2:]
    g = lax.axis_index("gene")
    for owner, out_ref in zip(owners(), outs):
        for j, piece in enumerate(pieces):
            out_ref[j] = pick_blocks(cols_ref, g ^ mask_of(owner), owner == 0, piece[:, :TILE], piece[:, TILE:])


def mask_of(s):
    mask = s * 0
    for at, value in enumerate(MASKS):
        mask = jnp.where(s == at, value, mask)
    return mask


def owners():
    s = lax.axis_index("sample")
    return s, s ^ PARTNER


def placed(tiles, columns):
    zero = jnp.zeros((TILE, TILE), BF)
    rows = [
        jnp.concatenate([jnp.where(column == c, tile.astype(BF), zero) for c in range(2)], axis=1)
        for tile, column in zip(tiles, columns)
    ]
    return jnp.concatenate(rows, axis=0)


def first_columns_kernel(
    cols_ref, counts_ref, far_ref, cross_ref, hub_ref, y_ref, tile_ref, slots_ref, sems
):
    s, g = lax.axis_index("sample"), lax.axis_index("gene")
    copies = [
        pltpu.make_async_copy(far_ref.at[h], slots_ref.at[h], sems.at[h]) for h in range(far_ref.shape[0])
    ]
    for copy in copies:
        copy.start()
    for p in range(2):
        tile_ref[p] = jnp.where(s == 0, hub_ref[p], cross_ref[g ^ mask_of(s), p])
    total = jnp.zeros(y_ref.shape, F32)
    for h in range(cross_ref.shape[0]):
        tiles = [jnp.where(h == g, hub_ref[p], cross_ref[h, p]) for p in range(2)]
        columns = [column_of(cols_ref, counts_ref, h, p) for p in range(2)]
        copies[h].wait()
        total += dot(slots_ref[h], placed(tiles, columns))
    y_ref[...] = total.astype(BF)


def position_of(j):
    back, other = order(ALL)[j]
    s = lax.axis_index("sample")
    chips = lax.axis_size("sample") // 2
    return lax.rem(s // 2 - back + chips, chips) * 2 + (s % 2 ^ other)


def peer_of(j):
    return lax.axis_index("gene") ^ mask_of(position_of(j))


def later_columns_kernel(cols_ref, counts_ref, slots_ref, *refs):
    pieces, y_ref = refs[:-1], refs[-1]
    total = jnp.zeros(y_ref.shape, F32)
    for j, piece in enumerate(pieces):
        h = peer_of(j)
        columns = [column_of(cols_ref, counts_ref, h, p) for p in range(2)]
        total += dot(slots_ref[h], placed([piece[p, :TILE] for p in range(2)], columns))
    y_ref[...] = total.astype(BF)


def gradient_kernel(cols_ref, counts_ref, own_rows_ref, partner_rows_ref, *refs):
    pieces, outs = refs[:-2], refs[-2:]
    g = lax.axis_index("gene")
    for owner, rows_ref, out_ref in zip(owners(), (own_rows_ref, partner_rows_ref), outs):
        total = jnp.zeros((2 * TILE, 2 * TILE), F32)
        for j, piece in enumerate(pieces):
            total += dot_over_rows(rows_ref[j], piece[...])
        for p in range(2):
            rows = total[p * TILE : (p + 1) * TILE]
            column = column_of(cols_ref, counts_ref, g ^ mask_of(owner), p)
            out_ref[p] = jnp.where(column == 1, rows[:, TILE:], rows[:, :TILE])


def proximal(tile, gradient, mirrored, diagonal, sample_total):
    symmetric = 0.5 * (gradient + mirrored.T) / sample_total
    stepped = tile - STEP * symmetric
    shrunk = jnp.where(
        stepped > 0, jnp.maximum(stepped - SHRINK, 0.0), jnp.minimum(stepped + SHRINK, 0.0)
    )
    barrier = 0.5 * (stepped + jnp.sqrt(stepped * stepped + 4.0 * STEP))
    return jnp.where(diagonal, barrier, shrunk)


def eye():
    shape = (TILE, TILE)
    return lax.broadcasted_iota(jnp.int32, shape, 0) == lax.broadcasted_iota(jnp.int32, shape, 1)


def step_kernel(sample_total, cols_ref, counts_ref, tile_ref, *refs):
    (own_ref, partner_ref, mirrored_ref, far_ref), riders = refs[:4], refs[4:-2]
    new_ref, low_ref = refs[-2:]
    s, g = lax.axis_index("sample"), lax.axis_index("gene")
    on_diagonal = jnp.where(s == 0, eye().astype(F32), 0.0) > 0.5
    for p in range(2):
        gradient, mirrored = own_ref[p] + partner_ref[p], mirrored_ref[p] + far_ref[p]
        new = proximal(tile_ref[p], gradient, mirrored, on_diagonal, sample_total)
        new = jnp.where(column_of(cols_ref, counts_ref, g ^ mask_of(s), p) < 2, new, 0.0)
        new_ref[p] = new
        low_ref[p, :TILE] = new.astype(BF)
        for rider in riders:
            low_ref[p, TILE:] = rider[p]


def upper(strict):
    shape = (TILE, TILE)
    row, column = lax.broadcasted_iota(jnp.int32, shape, 0), lax.broadcasted_iota(jnp.int32, shape, 1)
    return row < column if strict else row <= column


def chunk_at(s):
    return (s & 1) * 8 + (s & 2) * 2 + (s & 4) // 2 + (s & 8) // 8


def gram_kernel(x_ref, after_ref, keep_ref, send_ref, all_ref):
    here = chunk_at(lax.axis_index("sample"))
    half = keep_ref.shape[0]
    for b in range(2 * half):
        x = x_ref[:, 2 * b * TILE : 2 * (b + 1) * TILE]
        first, second = (dot_over_rows(x[:, at : at + TILE], x[:, at : at + TILE]) for at in (0, TILE))
        diagonal = jnp.sum(jnp.where(eye(), second, 0.0), axis=0, keepdims=True)
        at = chunk_at(b) ^ here
        all_ref[at, :TILE] = jnp.where(upper(False), first, second)
        all_ref[at, TILE:] = jnp.broadcast_to(diagonal, (EXTRA, TILE))
    keep_ref[...] = all_ref[:half]
    send_ref[...] = all_ref[half:].astype(BF)


def halve_kernel(kept_ref, received_ref, keep_ref, send_ref):
    half = keep_ref.shape[0]
    keep_ref[...] = kept_ref[:half] + received_ref[:half].astype(F32)
    send_ref[...] = (kept_ref[half:] + received_ref[half:].astype(F32)).astype(send_ref.dtype)


def diagonal_kernel(sample_total, kept_ref, received_ref, tiles_ref, out_ref, tile_ref, sem):
    first_tile = 2 * lax.axis_index("sample")
    copy = pltpu.make_async_copy(tiles_ref.at[pl.ds(first_tile, 2)], tile_ref, sem)
    copy.start()
    whole = kept_ref[0] + received_ref[0]
    packed = whole[:TILE]
    turned = packed.T
    first = jnp.where(upper(False), packed, turned)
    second = jnp.where(upper(True), turned, packed)
    second = jnp.where(eye(), whole[TILE : TILE + 1], second)
    copy.wait()
    for p, gram in enumerate((first, second)):
        high = gram.astype(BF)
        low = (gram - high.astype(F32)).astype(BF)
        tile = tile_ref[p]
        for _ in range(ITERS):
            lowered = tile.astype(BF)
            gradient = dot(high, lowered) + dot(low, lowered)
            tile = proximal(tile, gradient, gradient, eye(), sample_total)
        lowered = tile.astype(BF)
        rest = jnp.sum(jnp.where(eye(), tile - lowered.astype(F32), 0.0), axis=0, keepdims=True)
        out_ref[p, :TILE] = lowered
        out_ref[p, TILE:] = jnp.broadcast_to(rest, (EXTRA, TILE)).astype(BF)


def widen_kernel(*refs):
    pieces, out_ref = refs[:-1], refs[-1]
    for j, piece in enumerate(pieces):
        first = 2 * position_of(j)
        for p in range(2):
            rest = piece[p, 2 * TILE :].astype(F32)[:1]
            tile = piece[p, TILE : 2 * TILE].astype(F32)
            out_ref[first + p] = tile + jnp.where(eye(), rest, 0.0)


def assemble_kernel(*refs):
    pieces, (diag_in_ref, cross_ref, diag_ref, hub_ref, sem) = refs[:-5], refs[-5:]
    for j, piece in enumerate(pieces):
        h = peer_of(j)
        own = h == lax.axis_index("gene")
        for p in range(2):
            cross_ref[h, p] = jnp.where(own, 0.0, piece[p].astype(F32))

        @pl.when(own)
        def _():
            for p in range(2):
                hub_ref[p] = piece[p].astype(F32)

    copy = pltpu.make_async_copy(hub_ref, diag_ref.at[pl.ds(0, 2)], sem)
    copy.start()
    copy.wait()


def call(kernel, outs, spaces, *args, scratch=()):
    moved = sum(x.size * x.dtype.itemsize for x in list(args) + jax.tree.leaves(outs))
    return pl.pallas_call(
        kernel,
        out_shape=outs,
        in_specs=list(spaces) + [VMEM] * (len(args) - len(spaces)),
        out_specs=jax.tree.map(lambda _: VMEM, outs),
        compiler_params=PARAMS,
        scratch_shapes=scratch,
        cost_estimate=pl.CostEstimate(flops=10**8, bytes_accessed=moved, transcendentals=0),
    )(*args)


def shards(samples, diag_tiles, cross_tiles, peer_cols, pair_counts):
    s, g = lax.axis_index("sample"), lax.axis_index("gene")
    genes = lax.axis_size("gene")
    rows = samples.shape[0]
    sample_total = rows * lax.axis_size("sample")
    shape = jax.ShapeDtypeStruct
    cols, counts = peer_cols, pair_counts
    part = shape((rows, 2 * TILE), BF)

    hubs = samples[:, : 2 * TILE]
    row_shards = [hubs] + [shift_z(hubs, back) for back in PARITY[1:]]
    outgoing = call(
        outgoing_kernel,
        shape((genes,) + part.shape, BF),
        [SMEM] + [ANY] * len(row_shards[1:]),
        cols, *row_shards[1:], hubs,
    )
    slots = lax.all_to_all(outgoing, "gene", split_axis=0, concat_axis=0, tiled=True)
    rows_shape = shape((len(order(PARITY)),) + part.shape, BF)
    arranged = call(arrange_kernel, [rows_shape] * 2, [SMEM], cols, *row_shards, *[swap_core(x) for x in row_shards])
    own_rows = swap_owner(arranged[0], 0, lambda s: MASKS[s])
    partner_rows = swap_owner(arranged[1], 0, lambda s: MASKS[s ^ PARTNER])

    chunk = (TILE + EXTRA, TILE)
    count = diag_tiles.shape[0] // 2
    kept, sent = call(
        gram_kernel,
        [shape((count // 2,) + chunk, F32), shape((count // 2,) + chunk, BF)],
        [VMEM, ANY],
        samples, outgoing,
        scratch=[pltpu.VMEM((count,) + chunk, F32)],
    )
    received = swap_core(sent)
    for bit, dtype in ((2, BF), (4, F32), (8, F32)):
        half = (kept.shape[0] // 2,) + chunk
        kept, sent = call(halve_kernel, [shape(half, F32), shape(half, dtype)], [], kept, received)
        received = lax.ppermute(sent, "sample", [(i, i ^ bit) for i in range(lax.axis_size("sample"))])
    my_diag = call(
        functools.partial(diagonal_kernel, sample_total),
        shape((2,) + chunk, BF),
        [VMEM, VMEM, ANY],
        kept, received, diag_tiles,
        scratch=[pltpu.VMEM((2, TILE, TILE), F32), pltpu.SemaphoreType.DMA(())],
    )

    pair = (2, TILE, TILE)
    for iteration in range(ITERS):
        if iteration == 0:
            columns, tile = call(
                first_columns_kernel,
                [part, shape(pair, F32)],
                [SMEM, SMEM, ANY],
                cols, counts, slots, cross_tiles[0], diag_tiles[:2],
                scratch=[pltpu.VMEM(slots.shape, BF), pltpu.SemaphoreType.DMA((genes,))],
            )
        else:
            columns = call(later_columns_kernel, part, [SMEM, SMEM], cols, counts, slots, *pieces)
        own, partner = call(
            gradient_kernel,
            [shape(pair, F32)] * 2,
            [SMEM, SMEM],
            cols, counts, own_rows, partner_rows, *gather_shards(columns, PARITY),
        )
        others = (
            swap_owner(partner, PARTNER, lambda s: 0),
            swap_owner(own, 0, lambda s: MASKS[s]),
            swap_owner(partner, PARTNER, lambda s: MASKS[s ^ PARTNER]),
        )
        riders = [my_diag] if iteration == 0 else []
        tile, lowered = call(
            functools.partial(step_kernel, sample_total),
            [shape(pair, F32), shape((2, TILE + sum(r.shape[1] for r in riders), TILE), BF)],
            [SMEM, SMEM],
            cols, counts, tile, own, *others, *riders,
        )
        if iteration == 0:
            pieces = forward_shards(lowered)
            all_diag = call(widen_kernel, shape(diag_tiles.shape, F32), [], *pieces)
        else:
            pieces = gather_shards(lowered, ALL)

    cross, diag = pl.pallas_call(
        assemble_kernel,
        out_shape=[shape(cross_tiles.shape[1:], F32), shape(diag_tiles.shape, F32)],
        in_specs=[VMEM] * len(pieces) + [ANY],
        out_specs=[VMEM, ANY],
        scratch_shapes=[pltpu.VMEM(pair, F32), pltpu.SemaphoreType.DMA(())],
        input_output_aliases={len(pieces): 1},
        compiler_params=PARAMS,
    )(*pieces, all_diag)
    return diag, cross[None]


def solution(mesh):
    in_specs = (
        P("sample", "gene"),
        P("gene", None, None),
        P("gene", None, None, None, None),
        P("gene", None, None),
        P("gene", None),
    )
    out_specs = (P("gene", None, None), P("gene", None, None, None, None))
    return jax.shard_map(shards, mesh=mesh, in_specs=in_specs, out_specs=out_specs, check_vma=False)
```

```python
import functools

import jax
import jax.numpy as jnp
from jax import lax
from jax.experimental import pallas as pl
from jax.experimental.pallas import tpu as pltpu
from jax.sharding import PartitionSpec as P

ITERS = 2
STEP = 0.5
SHRINK = 0.02
TILE = 128
EXTRA = 16
BF = jnp.bfloat16
F32 = jnp.float32

ALL = (0, 1, -1, 2, -2, 3, -3, 4)
PARITY = (0, 2, -2, 4)
MASKS = tuple(
    4 * y + x
    for (x, y) in (
        (0, 0), (2, 2), (2, 0), (0, 2), (2, 1), (0, 3), (2, 3), (0, 1),
        (1, 0), (3, 2), (3, 0), (1, 2), (1, 1), (3, 3), (1, 3), (3, 1),
    )
)
PARTNER = 2


def order(backs):
    return tuple((back, other) for other in (0, 1) for back in backs)


VMEM = pl.BlockSpec(memory_space=pltpu.VMEM)
SMEM = pl.BlockSpec(memory_space=pltpu.SMEM)
ANY = pl.BlockSpec(memory_space=pl.ANY)
PARAMS = pltpu.CompilerParams(vmem_limit_bytes=48 * 1024 * 1024)


def shift_z(x, chips):
    count = lax.axis_size("sample")
    return lax.ppermute(x, "sample", [(i, (i + 2 * chips) % count) for i in range(count)])


def swap_core(x):
    count = lax.axis_size("sample")
    return lax.ppermute(x, "sample", [(i, i ^ 1) for i in range(count)])


def gather_shards(x, backs):
    own = [x] + [shift_z(x, back) for back in backs[1:]]
    return own + [swap_core(piece) for piece in own]


def forward_shards(x):
    up, down, up2, down2 = (shift_z(x, back) for back in (1, -1, 2, -2))
    half = x.shape[0] // 2
    far = jnp.concatenate([shift_z(up2[:half], 2), shift_z(down2[half:], -2)], axis=0)
    own = [x, up, down, up2, down2, shift_z(up2, 1), shift_z(down2, -1), far]
    return own + [swap_core(piece) for piece in own]


def swap_owner(x, sample_xor, gene_xor):
    samples, genes = lax.axis_size("sample"), lax.axis_size("gene")
    pairs = [
        (s * genes + g, (s ^ sample_xor) * genes + (g ^ gene_xor(s)))
        for s in range(samples)
        for g in range(genes)
    ]
    return lax.ppermute(x, ("sample", "gene"), pairs)


def dot(a, b):
    return jnp.dot(a, b, preferred_element_type=F32)


def dot_over_rows(a, b):
    return lax.dot_general(a, b, (((0,), (0,)), ((), ())), preferred_element_type=F32)


def column_of(cols_ref, counts_ref, h, p):
    live = jnp.where(p < counts_ref[0, h], cols_ref[0, h, p], 2)
    return jnp.where(h == lax.axis_index("gene"), p, live)


def pick_blocks(cols_ref, h, own, left, right):
    picks = [jnp.where(own, p, cols_ref[0, h, p]) for p in range(2)]
    return jnp.concatenate([jnp.where(pick == 1, right, left) for pick in picks], axis=-1)


def outgoing_kernel(cols_ref, x_ref, out_ref):
    left, right = x_ref[:, :TILE], x_ref[:, TILE:]
    for h in range(out_ref.shape[0]):
        out_ref[h] = pick_blocks(cols_ref, h, h == lax.axis_index("gene"), left, right)


def arrange_kernel(cols_ref, *refs):
    pieces, outs = refs[:-2], refs[-2:]
    g = lax.axis_index("gene")
    for owner, out_ref in zip(owners(), outs):
        for j, piece in enumerate(pieces):
            out_ref[j] = pick_blocks(cols_ref, g ^ mask_of(owner), owner == 0, piece[:, :TILE], piece[:, TILE:])


def mask_of(s):
    mask = s * 0
    for at, value in enumerate(MASKS):
        mask = jnp.where(s == at, value, mask)
    return mask


def owners():
    s = lax.axis_index("sample")
    return s, s ^ PARTNER


def placed(tiles, columns):
    zero = jnp.zeros((TILE, TILE), BF)
    rows = [
        jnp.concatenate([jnp.where(column == c, tile.astype(BF), zero) for c in range(2)], axis=1)
        for tile, column in zip(tiles, columns)
    ]
    return jnp.concatenate(rows, axis=0)


def first_columns_kernel(cols_ref, counts_ref, slots_ref, cross_ref, hub_ref, y_ref, tile_ref):
    s, g = lax.axis_index("sample"), lax.axis_index("gene")
    for p in range(2):
        tile_ref[p] = jnp.where(s == 0, hub_ref[p], cross_ref[g ^ mask_of(s), p])
    total = jnp.zeros(y_ref.shape, F32)
    for h in range(cross_ref.shape[0]):
        tiles = [jnp.where(h == g, hub_ref[p], cross_ref[h, p]) for p in range(2)]
        columns = [column_of(cols_ref, counts_ref, h, p) for p in range(2)]
        total += dot(slots_ref[h], placed(tiles, columns))
    y_ref[...] = total.astype(BF)


def position_of(j):
    back, other = order(ALL)[j]
    s = lax.axis_index("sample")
    chips = lax.axis_size("sample") // 2
    return lax.rem(s // 2 - back + chips, chips) * 2 + (s % 2 ^ other)


def peer_of(j):
    return lax.axis_index("gene") ^ mask_of(position_of(j))


def later_columns_kernel(cols_ref, counts_ref, after_ref, slots_ref, *refs):
    pieces, y_ref = refs[:-1], refs[-1]
    total = jnp.zeros(y_ref.shape, F32)
    for j, piece in enumerate(pieces):
        h = peer_of(j)
        columns = [column_of(cols_ref, counts_ref, h, p) for p in range(2)]
        total += dot(slots_ref[h], placed([piece[p, :TILE] for p in range(2)], columns))
    y_ref[...] = total.astype(BF)


def gradient_kernel(cols_ref, counts_ref, own_rows_ref, partner_rows_ref, *refs):
    pieces, outs = refs[:-2], refs[-2:]
    g = lax.axis_index("gene")
    for owner, rows_ref, out_ref in zip(owners(), (own_rows_ref, partner_rows_ref), outs):
        total = jnp.zeros((2 * TILE, 2 * TILE), F32)
        for j, piece in enumerate(pieces):
            total += dot_over_rows(rows_ref[j], piece[...])
        for p in range(2):
            rows = total[p * TILE : (p + 1) * TILE]
            column = column_of(cols_ref, counts_ref, g ^ mask_of(owner), p)
            out_ref[p] = jnp.where(column == 1, rows[:, TILE:], rows[:, :TILE])


def proximal(tile, gradient, mirrored, diagonal, sample_total):
    symmetric = 0.5 * (gradient + mirrored.T) / sample_total
    stepped = tile - STEP * symmetric
    shrunk = jnp.where(
        stepped > 0, jnp.maximum(stepped - SHRINK, 0.0), jnp.minimum(stepped + SHRINK, 0.0)
    )
    barrier = 0.5 * (stepped + jnp.sqrt(stepped * stepped + 4.0 * STEP))
    return jnp.where(diagonal, barrier, shrunk)


def eye():
    shape = (TILE, TILE)
    return lax.broadcasted_iota(jnp.int32, shape, 0) == lax.broadcasted_iota(jnp.int32, shape, 1)


def step_kernel(sample_total, cols_ref, counts_ref, tile_ref, *refs):
    (own_ref, partner_ref, mirrored_ref, far_ref), riders = refs[:4], refs[4:-2]
    new_ref, low_ref = refs[-2:]
    s, g = lax.axis_index("sample"), lax.axis_index("gene")
    on_diagonal = jnp.where(s == 0, eye().astype(F32), 0.0) > 0.5
    for p in range(2):
        gradient, mirrored = own_ref[p] + partner_ref[p], mirrored_ref[p] + far_ref[p]
        new = proximal(tile_ref[p], gradient, mirrored, on_diagonal, sample_total)
        new = jnp.where(column_of(cols_ref, counts_ref, g ^ mask_of(s), p) < 2, new, 0.0)
        new_ref[p] = new
        low_ref[p, :TILE] = new.astype(BF)
        for rider in riders:
            low_ref[p, TILE:] = rider[p]


def upper(strict):
    shape = (TILE, TILE)
    row, column = lax.broadcasted_iota(jnp.int32, shape, 0), lax.broadcasted_iota(jnp.int32, shape, 1)
    return row < column if strict else row <= column


def chunk_at(s):
    return (s & 1) * 8 + (s & 2) * 2 + (s & 4) // 2 + (s & 8) // 8


def gram_kernel(x_ref, after_ref, cross_ref, keep_ref, send_ref, all_ref):
    here = chunk_at(lax.axis_index("sample"))
    half = keep_ref.shape[0]
    for b in range(2 * half):
        x = x_ref[:, 2 * b * TILE : 2 * (b + 1) * TILE]
        first, second = (dot_over_rows(x[:, at : at + TILE], x[:, at : at + TILE]) for at in (0, TILE))
        diagonal = jnp.sum(jnp.where(eye(), second, 0.0), axis=0, keepdims=True)
        at = chunk_at(b) ^ here
        all_ref[at, :TILE] = jnp.where(upper(False), first, second)
        all_ref[at, TILE:] = jnp.broadcast_to(diagonal, (EXTRA, TILE))
    keep_ref[...] = all_ref[:half]
    send_ref[...] = all_ref[half:].astype(BF)


def halve_kernel(kept_ref, received_ref, keep_ref, send_ref):
    half = keep_ref.shape[0]
    keep_ref[...] = kept_ref[:half] + received_ref[:half].astype(F32)
    send_ref[...] = (kept_ref[half:] + received_ref[half:].astype(F32)).astype(send_ref.dtype)


def diagonal_kernel(sample_total, kept_ref, received_ref, tiles_ref, out_ref, tile_ref, sem):
    first_tile = 2 * lax.axis_index("sample")
    copy = pltpu.make_async_copy(tiles_ref.at[pl.ds(first_tile, 2)], tile_ref, sem)
    copy.start()
    whole = kept_ref[0] + received_ref[0]
    packed = whole[:TILE]
    turned = packed.T
    first = jnp.where(upper(False), packed, turned)
    second = jnp.where(upper(True), turned, packed)
    second = jnp.where(eye(), whole[TILE : TILE + 1], second)
    copy.wait()
    for p, gram in enumerate((first, second)):
        high = gram.astype(BF)
        low = (gram - high.astype(F32)).astype(BF)
        tile = tile_ref[p]
        for _ in range(ITERS):
            lowered = tile.astype(BF)
            gradient = dot(high, lowered) + dot(low, lowered)
            tile = proximal(tile, gradient, gradient, eye(), sample_total)
        lowered = tile.astype(BF)
        rest = jnp.sum(jnp.where(eye(), tile - lowered.astype(F32), 0.0), axis=0, keepdims=True)
        out_ref[p, :TILE] = lowered
        out_ref[p, TILE:] = jnp.broadcast_to(rest, (EXTRA, TILE)).astype(BF)


def assemble_kernel(*refs):
    pieces, (cross_ref, diag_ref, cross_part, diag_part, cross_sems, diag_sems) = refs[:-6], refs[-6:]
    copies = []
    for j, piece in enumerate(pieces):
        at = position_of(j)
        for p in range(2):
            tile = piece[p, :TILE].astype(F32)
            rest = piece[p, 2 * TILE :].astype(F32)[:1]
            rider = piece[p, TILE : 2 * TILE].astype(F32) + jnp.where(eye(), rest, 0.0)
            cross_part[j, p] = jnp.where(at == 0, 0.0, tile)
            diag_part[j, p] = jnp.where(at == 0, tile, rider)
        copies += [
            pltpu.make_async_copy(cross_part.at[j], cross_ref.at[peer_of(j)], cross_sems.at[j]),
            pltpu.make_async_copy(diag_part.at[j], diag_ref.at[pl.ds(2 * at, 2)], diag_sems.at[j]),
        ]
        for copy in copies[-2:]:
            copy.start()
    for copy in copies:
        copy.wait()


def call(kernel, outs, spaces, *args, scratch=()):
    moved = sum(x.size * x.dtype.itemsize for x in list(args) + jax.tree.leaves(outs))
    return pl.pallas_call(
        kernel,
        out_shape=outs,
        in_specs=list(spaces) + [VMEM] * (len(args) - len(spaces)),
        out_specs=jax.tree.map(lambda _: VMEM, outs),
        compiler_params=PARAMS,
        scratch_shapes=scratch,
        cost_estimate=pl.CostEstimate(flops=10**8, bytes_accessed=moved, transcendentals=0),
    )(*args)


def shards(samples, diag_tiles, cross_tiles, peer_cols, pair_counts):
    s, g = lax.axis_index("sample"), lax.axis_index("gene")
    genes = lax.axis_size("gene")
    rows = samples.shape[0]
    sample_total = rows * lax.axis_size("sample")
    shape = jax.ShapeDtypeStruct
    cols, counts = peer_cols, pair_counts
    part = shape((rows, 2 * TILE), BF)

    hubs = samples[:, : 2 * TILE]
    outgoing = call(outgoing_kernel, shape((genes,) + part.shape, BF), [SMEM], cols, hubs)
    slots = lax.all_to_all(outgoing, "gene", split_axis=0, concat_axis=0, tiled=True)
    rows_shape = shape((len(order(PARITY)),) + part.shape, BF)
    arranged = call(arrange_kernel, [rows_shape] * 2, [SMEM], cols, *gather_shards(hubs, PARITY))
    own_rows = swap_owner(arranged[0], 0, lambda s: MASKS[s])
    partner_rows = swap_owner(arranged[1], 0, lambda s: MASKS[s ^ PARTNER])

    chunk = (TILE + EXTRA, TILE)
    count = diag_tiles.shape[0] // 2
    kept, sent = call(
        gram_kernel,
        [shape((count // 2,) + chunk, F32), shape((count // 2,) + chunk, BF)],
        [VMEM, ANY],
        samples, outgoing, cross_tiles[0],
        scratch=[pltpu.VMEM((count,) + chunk, F32)],
    )
    received = swap_core(sent)
    for bit, dtype in ((2, BF), (4, F32), (8, F32)):
        half = (kept.shape[0] // 2,) + chunk
        kept, sent = call(halve_kernel, [shape(half, F32), shape(half, dtype)], [], kept, received)
        received = lax.ppermute(sent, "sample", [(i, i ^ bit) for i in range(lax.axis_size("sample"))])
    my_diag = call(
        functools.partial(diagonal_kernel, sample_total),
        shape((2,) + chunk, BF),
        [VMEM, VMEM, ANY],
        kept, received, diag_tiles,
        scratch=[pltpu.VMEM((2, TILE, TILE), F32), pltpu.SemaphoreType.DMA(())],
    )

    pair = (2, TILE, TILE)
    for iteration in range(ITERS):
        if iteration == 0:
            columns, tile = call(
                first_columns_kernel,
                [part, shape(pair, F32)],
                [SMEM, SMEM],
                cols, counts, slots, cross_tiles[0], diag_tiles[:2],
            )
        else:
            columns = call(
                later_columns_kernel, part, [SMEM, SMEM, ANY], cols, counts, my_diag, slots, *pieces
            )
        own, partner = call(
            gradient_kernel,
            [shape(pair, F32)] * 2,
            [SMEM, SMEM],
            cols, counts, own_rows, partner_rows, *gather_shards(columns, PARITY),
        )
        others = (
            swap_owner(partner, PARTNER, lambda s: 0),
            swap_owner(own, 0, lambda s: MASKS[s]),
            swap_owner(partner, PARTNER, lambda s: MASKS[s ^ PARTNER]),
        )
        riders = [my_diag] if iteration == ITERS - 1 else []
        tile, lowered = call(
            functools.partial(step_kernel, sample_total),
            [shape(pair, F32), shape((2, TILE + sum(r.shape[1] for r in riders), TILE), BF)],
            [SMEM, SMEM],
            cols, counts, tile, own, *others, *riders,
        )
        pieces = forward_shards(lowered) if riders else gather_shards(lowered, ALL)

    place = pl.BlockSpec(memory_space=pl.ANY)
    chunk = pltpu.VMEM((len(pieces),) + pair, F32)
    cross, diag = pl.pallas_call(
        assemble_kernel,
        out_shape=[shape(cross_tiles.shape[1:], F32), shape(diag_tiles.shape, F32)],
        in_specs=[VMEM] * len(pieces),
        out_specs=[place, place],
        scratch_shapes=[chunk, chunk] + [pltpu.SemaphoreType.DMA((len(pieces),))] * 2,
        compiler_params=PARAMS,
    )(*pieces)
    return diag, cross[None]


def solution(mesh):
    in_specs = (
        P("sample", "gene"),
        P("gene", None, None),
        P("gene", None, None, None, None),
        P("gene", None, None),
        P("gene", None),
    )
    out_specs = (P("gene", None, None), P("gene", None, None, None, None))
    return jax.shard_map(shards, mesh=mesh, in_specs=in_specs, out_specs=out_specs, check_vma=False)
```

```python
import functools

import jax
import jax.numpy as jnp
from jax import lax
from jax.experimental import pallas as pl
from jax.experimental.pallas import tpu as pltpu
from jax.sharding import PartitionSpec as P

ITERS = 2
STEP = 0.5
SHRINK = 0.02
TILE = 128
EXTRA = 16
BF = jnp.bfloat16
F32 = jnp.float32

ALL = (0, 1, -1, 2, -2, 3, -3, 4)
PARITY = (0, 2, -2, 4)
MASKS = tuple(
    4 * y + x
    for (x, y) in (
        (0, 0), (2, 2), (2, 0), (0, 2), (2, 1), (0, 3), (2, 3), (0, 1),
        (1, 0), (3, 2), (3, 0), (1, 2), (1, 1), (3, 3), (1, 3), (3, 1),
    )
)
PARTNER = 2


def order(backs):
    return tuple((back, other) for other in (0, 1) for back in backs)


VMEM = pl.BlockSpec(memory_space=pltpu.VMEM)
SMEM = pl.BlockSpec(memory_space=pltpu.SMEM)
ANY = pl.BlockSpec(memory_space=pl.ANY)
PARAMS = pltpu.CompilerParams(vmem_limit_bytes=48 * 1024 * 1024)


def shift_z(x, chips):
    count = lax.axis_size("sample")
    return lax.ppermute(x, "sample", [(i, (i + 2 * chips) % count) for i in range(count)])


def swap_core(x):
    count = lax.axis_size("sample")
    return lax.ppermute(x, "sample", [(i, i ^ 1) for i in range(count)])


def gather_shards(x, backs):
    own = [x] + [shift_z(x, back) for back in backs[1:]]
    return own + [swap_core(piece) for piece in own]


def forward_shards(x):
    up, down, up2, down2 = (shift_z(x, back) for back in (1, -1, 2, -2))
    half = x.shape[0] // 2
    far = jnp.concatenate([shift_z(up2[:half], 2), shift_z(down2[half:], -2)], axis=0)
    own = [x, up, down, up2, down2, shift_z(up2, 1), shift_z(down2, -1), far]
    return own + [swap_core(piece) for piece in own]


def swap_owner(x, sample_xor, gene_xor):
    samples, genes = lax.axis_size("sample"), lax.axis_size("gene")
    pairs = [
        (s * genes + g, (s ^ sample_xor) * genes + (g ^ gene_xor(s)))
        for s in range(samples)
        for g in range(genes)
    ]
    return lax.ppermute(x, ("sample", "gene"), pairs)


def dot(a, b):
    return jnp.dot(a, b, preferred_element_type=F32)


def dot_over_rows(a, b):
    return lax.dot_general(a, b, (((0,), (0,)), ((), ())), preferred_element_type=F32)


def column_of(cols_ref, counts_ref, h, p):
    live = jnp.where(p < counts_ref[0, h], cols_ref[0, h, p], 2)
    return jnp.where(h == lax.axis_index("gene"), p, live)


def pick_blocks(cols_ref, h, own, left, right):
    picks = [jnp.where(own, p, cols_ref[0, h, p]) for p in range(2)]
    return jnp.concatenate([jnp.where(pick == 1, right, left) for pick in picks], axis=-1)


def outgoing_kernel(cols_ref, x_ref, out_ref):
    left, right = x_ref[:, :TILE], x_ref[:, TILE:]
    for h in range(out_ref.shape[0]):
        out_ref[h] = pick_blocks(cols_ref, h, h == lax.axis_index("gene"), left, right)


def arrange_kernel(cols_ref, *refs):
    pieces, outs = refs[:-2], refs[-2:]
    g = lax.axis_index("gene")
    for owner, out_ref in zip(owners(), outs):
        for j, piece in enumerate(pieces):
            out_ref[j] = pick_blocks(cols_ref, g ^ mask_of(owner), owner == 0, piece[:, :TILE], piece[:, TILE:])


def mask_of(s):
    mask = s * 0
    for at, value in enumerate(MASKS):
        mask = jnp.where(s == at, value, mask)
    return mask


def owners():
    s = lax.axis_index("sample")
    return s, s ^ PARTNER


def placed(tiles, columns):
    zero = jnp.zeros((TILE, TILE), BF)
    rows = [
        jnp.concatenate([jnp.where(column == c, tile.astype(BF), zero) for c in range(2)], axis=1)
        for tile, column in zip(tiles, columns)
    ]
    return jnp.concatenate(rows, axis=0)


def first_columns_kernel(
    cols_ref, counts_ref, slots_ref, cross_ref, diag_ref, y_ref, tile_ref, hub_ref, sem
):
    s, g = lax.axis_index("sample"), lax.axis_index("gene")
    copy = pltpu.make_async_copy(diag_ref.at[pl.ds(0, 2)], hub_ref, sem)
    copy.start()
    total = jnp.zeros(y_ref.shape, F32)
    for h in range(cross_ref.shape[0]):
        columns = [jnp.where(h == g, 2, column_of(cols_ref, counts_ref, h, p)) for p in range(2)]
        total += dot(slots_ref[h], placed([cross_ref[h, p] for p in range(2)], columns))
    copy.wait()
    total += dot(slots_ref[g], placed([hub_ref[p] for p in range(2)], range(2)))
    y_ref[...] = total.astype(BF)
    for p in range(2):
        tile_ref[p] = jnp.where(s == 0, hub_ref[p], cross_ref[g ^ mask_of(s), p])


def position_of(j):
    back, other = order(ALL)[j]
    s = lax.axis_index("sample")
    chips = lax.axis_size("sample") // 2
    return lax.rem(s // 2 - back + chips, chips) * 2 + (s % 2 ^ other)


def peer_of(j):
    return lax.axis_index("gene") ^ mask_of(position_of(j))


def later_columns_kernel(cols_ref, counts_ref, slots_ref, *refs):
    pieces, y_ref = refs[:-1], refs[-1]
    total = jnp.zeros(y_ref.shape, F32)
    for j, piece in enumerate(pieces):
        h = peer_of(j)
        columns = [column_of(cols_ref, counts_ref, h, p) for p in range(2)]
        total += dot(slots_ref[h], placed([piece[p, :TILE] for p in range(2)], columns))
    y_ref[...] = total.astype(BF)


def gradient_kernel(cols_ref, counts_ref, after_ref, own_rows_ref, partner_rows_ref, *refs):
    pieces, outs = refs[:-2], refs[-2:]
    g = lax.axis_index("gene")
    for owner, rows_ref, out_ref in zip(owners(), (own_rows_ref, partner_rows_ref), outs):
        total = jnp.zeros((2 * TILE, 2 * TILE), F32)
        for j, piece in enumerate(pieces):
            total += dot_over_rows(rows_ref[j], piece[...])
        for p in range(2):
            rows = total[p * TILE : (p + 1) * TILE]
            column = column_of(cols_ref, counts_ref, g ^ mask_of(owner), p)
            out_ref[p] = jnp.where(column == 1, rows[:, TILE:], rows[:, :TILE])


def proximal(tile, gradient, mirrored, diagonal, sample_total):
    symmetric = 0.5 * (gradient + mirrored.T) / sample_total
    stepped = tile - STEP * symmetric
    shrunk = jnp.where(
        stepped > 0, jnp.maximum(stepped - SHRINK, 0.0), jnp.minimum(stepped + SHRINK, 0.0)
    )
    barrier = 0.5 * (stepped + jnp.sqrt(stepped * stepped + 4.0 * STEP))
    return jnp.where(diagonal, barrier, shrunk)


def eye():
    shape = (TILE, TILE)
    return lax.broadcasted_iota(jnp.int32, shape, 0) == lax.broadcasted_iota(jnp.int32, shape, 1)


def step_kernel(sample_total, cols_ref, counts_ref, tile_ref, *refs):
    (own_ref, partner_ref, mirrored_ref, far_ref), riders = refs[:4], refs[4:-2]
    new_ref, low_ref = refs[-2:]
    s, g = lax.axis_index("sample"), lax.axis_index("gene")
    on_diagonal = jnp.where(s == 0, eye().astype(F32), 0.0) > 0.5
    for p in range(2):
        gradient, mirrored = own_ref[p] + partner_ref[p], mirrored_ref[p] + far_ref[p]
        new = proximal(tile_ref[p], gradient, mirrored, on_diagonal, sample_total)
        new = jnp.where(column_of(cols_ref, counts_ref, g ^ mask_of(s), p) < 2, new, 0.0)
        new_ref[p] = new
        low_ref[p, :TILE] = new.astype(BF)
        for rider in riders:
            low_ref[p, TILE:] = rider[p]


def upper(strict):
    shape = (TILE, TILE)
    row, column = lax.broadcasted_iota(jnp.int32, shape, 0), lax.broadcasted_iota(jnp.int32, shape, 1)
    return row < column if strict else row <= column


def chunk_at(s):
    return (s & 1) * 8 + (s & 2) * 2 + (s & 4) // 2 + (s & 8) // 8


def gram_kernel(x_ref, after_ref, keep_ref, send_ref, all_ref):
    here = chunk_at(lax.axis_index("sample"))
    half = keep_ref.shape[0]
    for b in range(2 * half):
        x = x_ref[:, 2 * b * TILE : 2 * (b + 1) * TILE]
        first, second = (dot_over_rows(x[:, at : at + TILE], x[:, at : at + TILE]) for at in (0, TILE))
        diagonal = jnp.sum(jnp.where(eye(), second, 0.0), axis=0, keepdims=True)
        at = chunk_at(b) ^ here
        all_ref[at, :TILE] = jnp.where(upper(False), first, second)
        all_ref[at, TILE:] = jnp.broadcast_to(diagonal, (EXTRA, TILE))
    keep_ref[...] = all_ref[:half]
    send_ref[...] = all_ref[half:].astype(BF)


def halve_kernel(kept_ref, received_ref, keep_ref, send_ref):
    half = keep_ref.shape[0]
    keep_ref[...] = kept_ref[:half] + received_ref[:half].astype(F32)
    send_ref[...] = (kept_ref[half:] + received_ref[half:].astype(F32)).astype(send_ref.dtype)


def diagonal_kernel(sample_total, kept_ref, received_ref, tiles_ref, out_ref, tile_ref, sem):
    first_tile = 2 * lax.axis_index("sample")
    copy = pltpu.make_async_copy(tiles_ref.at[pl.ds(first_tile, 2)], tile_ref, sem)
    copy.start()
    whole = kept_ref[0] + received_ref[0]
    packed = whole[:TILE]
    turned = packed.T
    first = jnp.where(upper(False), packed, turned)
    second = jnp.where(upper(True), turned, packed)
    second = jnp.where(eye(), whole[TILE : TILE + 1], second)
    copy.wait()
    for p, gram in enumerate((first, second)):
        high = gram.astype(BF)
        low = (gram - high.astype(F32)).astype(BF)
        tile = tile_ref[p]
        for _ in range(ITERS):
            lowered = tile.astype(BF)
            gradient = dot(high, lowered) + dot(low, lowered)
            tile = proximal(tile, gradient, gradient, eye(), sample_total)
        lowered = tile.astype(BF)
        rest = jnp.sum(jnp.where(eye(), tile - lowered.astype(F32), 0.0), axis=0, keepdims=True)
        out_ref[p, :TILE] = lowered
        out_ref[p, TILE:] = jnp.broadcast_to(rest, (EXTRA, TILE)).astype(BF)


def assemble_kernel(*refs):
    pieces, (cross_ref, diag_ref, cross_part, diag_part, cross_sems, diag_sems) = refs[:-6], refs[-6:]
    copies = []
    for j, piece in enumerate(pieces):
        at = position_of(j)
        for p in range(2):
            tile = piece[p, :TILE].astype(F32)
            rest = piece[p, 2 * TILE :].astype(F32)[:1]
            rider = piece[p, TILE : 2 * TILE].astype(F32) + jnp.where(eye(), rest, 0.0)
            cross_part[j, p] = jnp.where(at == 0, 0.0, tile)
            diag_part[j, p] = jnp.where(at == 0, tile, rider)
        copies += [
            pltpu.make_async_copy(cross_part.at[j], cross_ref.at[peer_of(j)], cross_sems.at[j]),
            pltpu.make_async_copy(diag_part.at[j], diag_ref.at[pl.ds(2 * at, 2)], diag_sems.at[j]),
        ]
        for copy in copies[-2:]:
            copy.start()
    for copy in copies:
        copy.wait()


def call(kernel, outs, spaces, *args, scratch=()):
    moved = sum(x.size * x.dtype.itemsize for x in list(args) + jax.tree.leaves(outs))
    return pl.pallas_call(
        kernel,
        out_shape=outs,
        in_specs=list(spaces) + [VMEM] * (len(args) - len(spaces)),
        out_specs=jax.tree.map(lambda _: VMEM, outs),
        compiler_params=PARAMS,
        scratch_shapes=scratch,
        cost_estimate=pl.CostEstimate(flops=10**8, bytes_accessed=moved, transcendentals=0),
    )(*args)


def shards(samples, diag_tiles, cross_tiles, peer_cols, pair_counts):
    s, g = lax.axis_index("sample"), lax.axis_index("gene")
    genes = lax.axis_size("gene")
    rows = samples.shape[0]
    sample_total = rows * lax.axis_size("sample")
    shape = jax.ShapeDtypeStruct
    cols, counts = peer_cols, pair_counts
    part = shape((rows, 2 * TILE), BF)

    hubs = samples[:, : 2 * TILE]
    outgoing = call(outgoing_kernel, shape((genes,) + part.shape, BF), [SMEM], cols, hubs)
    slots = lax.all_to_all(outgoing, "gene", split_axis=0, concat_axis=0, tiled=True)
    rows_shape = shape((len(order(PARITY)),) + part.shape, BF)
    arranged = call(arrange_kernel, [rows_shape] * 2, [SMEM], cols, *gather_shards(hubs, PARITY))
    own_rows = swap_owner(arranged[0], 0, lambda s: MASKS[s])
    partner_rows = swap_owner(arranged[1], 0, lambda s: MASKS[s ^ PARTNER])

    pair = (2, TILE, TILE)
    for iteration in range(ITERS):
        if iteration == 0:
            columns, tile = call(
                first_columns_kernel,
                [part, shape(pair, F32)],
                [SMEM, SMEM, VMEM, VMEM, ANY],
                cols, counts, slots, cross_tiles[0], diag_tiles,
                scratch=[pltpu.VMEM(pair, F32), pltpu.SemaphoreType.DMA(())],
            )
            chunk = (TILE + EXTRA, TILE)
            count = diag_tiles.shape[0] // 2
            kept, sent = call(
                gram_kernel,
                [shape((count // 2,) + chunk, F32), shape((count // 2,) + chunk, BF)],
                [VMEM, ANY],
                samples, columns,
                scratch=[pltpu.VMEM((count,) + chunk, F32)],
            )
            received = swap_core(sent)
            for bit, dtype in ((2, BF), (4, F32), (8, F32)):
                half = (kept.shape[0] // 2,) + chunk
                kept, sent = call(halve_kernel, [shape(half, F32), shape(half, dtype)], [], kept, received)
                received = lax.ppermute(sent, "sample", [(i, i ^ bit) for i in range(lax.axis_size("sample"))])
            my_diag = call(
                functools.partial(diagonal_kernel, sample_total),
                shape((2,) + chunk, BF),
                [VMEM, VMEM, ANY],
                kept, received, diag_tiles,
                scratch=[pltpu.VMEM((2, TILE, TILE), F32), pltpu.SemaphoreType.DMA(())],
            )
        else:
            columns = call(later_columns_kernel, part, [SMEM, SMEM], cols, counts, slots, *pieces)
        own, partner = call(
            gradient_kernel,
            [shape(pair, F32)] * 2,
            [SMEM, SMEM, ANY],
            cols, counts, my_diag if iteration else columns, own_rows, partner_rows,
            *gather_shards(columns, PARITY),
        )
        others = (
            swap_owner(partner, PARTNER, lambda s: 0),
            swap_owner(own, 0, lambda s: MASKS[s]),
            swap_owner(partner, PARTNER, lambda s: MASKS[s ^ PARTNER]),
        )
        riders = [my_diag] if iteration == ITERS - 1 else []
        tile, lowered = call(
            functools.partial(step_kernel, sample_total),
            [shape(pair, F32), shape((2, TILE + sum(r.shape[1] for r in riders), TILE), BF)],
            [SMEM, SMEM],
            cols, counts, tile, own, *others, *riders,
        )
        pieces = forward_shards(lowered) if riders else gather_shards(lowered, ALL)

    place = pl.BlockSpec(memory_space=pl.ANY)
    chunk = pltpu.VMEM((len(pieces),) + pair, F32)
    cross, diag = pl.pallas_call(
        assemble_kernel,
        out_shape=[shape(cross_tiles.shape[1:], F32), shape(diag_tiles.shape, F32)],
        in_specs=[VMEM] * len(pieces),
        out_specs=[place, place],
        scratch_shapes=[chunk, chunk] + [pltpu.SemaphoreType.DMA((len(pieces),))] * 2,
        compiler_params=PARAMS,
    )(*pieces)
    return diag, cross[None]


def solution(mesh):
    in_specs = (
        P("sample", "gene"),
        P("gene", None, None),
        P("gene", None, None, None, None),
        P("gene", None, None),
        P("gene", None),
    )
    out_specs = (P("gene", None, None), P("gene", None, None, None, None))
    return jax.shard_map(shards, mesh=mesh, in_specs=in_specs, out_specs=out_specs, check_vma=False)
```

```python
import functools

import jax
import jax.numpy as jnp
from jax import lax
from jax.experimental import pallas as pl
from jax.experimental.pallas import tpu as pltpu
from jax.sharding import PartitionSpec as P

ITERS = 2
STEP = 0.5
SHRINK = 0.02
TILE = 128
EXTRA = 16
BF = jnp.bfloat16
F32 = jnp.float32

ALL = (0, 1, -1, 2, -2, 3, -3, 4)
PARITY = (0, 2, -2, 4)
MASKS = tuple(
    4 * y + x
    for (x, y) in (
        (0, 0), (2, 2), (2, 0), (0, 2), (2, 1), (0, 3), (2, 3), (0, 1),
        (1, 0), (3, 2), (3, 0), (1, 2), (1, 1), (3, 3), (1, 3), (3, 1),
    )
)
PARTNER = 2


def order(backs):
    return tuple((back, other) for other in (0, 1) for back in backs)


VMEM = pl.BlockSpec(memory_space=pltpu.VMEM)
SMEM = pl.BlockSpec(memory_space=pltpu.SMEM)
ANY = pl.BlockSpec(memory_space=pl.ANY)
PARAMS = pltpu.CompilerParams(vmem_limit_bytes=16 * 1024 * 1024)


def shift_z(x, chips):
    count = lax.axis_size("sample")
    return lax.ppermute(x, "sample", [(i, (i + 2 * chips) % count) for i in range(count)])


def swap_core(x):
    count = lax.axis_size("sample")
    return lax.ppermute(x, "sample", [(i, i ^ 1) for i in range(count)])


def gather_shards(x, backs):
    own = [x] + [shift_z(x, back) for back in backs[1:]]
    return own + [swap_core(piece) for piece in own]


def forward_shards(x):
    up, down, up2, down2 = (shift_z(x, back) for back in (1, -1, 2, -2))
    half = x.shape[0] // 2
    far = jnp.concatenate([shift_z(up2[:half], 2), shift_z(down2[half:], -2)], axis=0)
    own = [x, up, down, up2, down2, shift_z(up2, 1), shift_z(down2, -1), far]
    return own + [swap_core(piece) for piece in own]


def swap_owner(x, sample_xor, gene_xor):
    samples, genes = lax.axis_size("sample"), lax.axis_size("gene")
    pairs = [
        (s * genes + g, (s ^ sample_xor) * genes + (g ^ gene_xor(s)))
        for s in range(samples)
        for g in range(genes)
    ]
    return lax.ppermute(x, ("sample", "gene"), pairs)


def dot(a, b):
    return jnp.dot(a, b, preferred_element_type=F32)


def dot_over_rows(a, b):
    return lax.dot_general(a, b, (((0,), (0,)), ((), ())), preferred_element_type=F32)


def column_of(cols_ref, counts_ref, h, p):
    live = jnp.where(p < counts_ref[0, h], cols_ref[0, h, p], 2)
    return jnp.where(h == lax.axis_index("gene"), p, live)


def pick_blocks(cols_ref, h, own, left, right):
    picks = [jnp.where(own, p, cols_ref[0, h, p]) for p in range(2)]
    return jnp.concatenate([jnp.where(pick == 1, right, left) for pick in picks], axis=-1)


def outgoing_kernel(cols_ref, x_ref, out_ref):
    left, right = x_ref[:, :TILE], x_ref[:, TILE:]
    for h in range(out_ref.shape[0]):
        out_ref[h] = pick_blocks(cols_ref, h, h == lax.axis_index("gene"), left, right)


def arrange_kernel(cols_ref, *refs):
    pieces, outs = refs[:-2], refs[-2:]
    g = lax.axis_index("gene")
    for owner, out_ref in zip(owners(), outs):
        for j, piece in enumerate(pieces):
            out_ref[j] = pick_blocks(cols_ref, g ^ mask_of(owner), owner == 0, piece[:, :TILE], piece[:, TILE:])


def mask_of(s):
    mask = s * 0
    for at, value in enumerate(MASKS):
        mask = jnp.where(s == at, value, mask)
    return mask


def owners():
    s = lax.axis_index("sample")
    return s, s ^ PARTNER


def placed(tiles, columns):
    zero = jnp.zeros((TILE, TILE), BF)
    rows = [
        jnp.concatenate([jnp.where(column == c, tile.astype(BF), zero) for c in range(2)], axis=1)
        for tile, column in zip(tiles, columns)
    ]
    return jnp.concatenate(rows, axis=0)


def first_columns_kernel(
    cols_ref, counts_ref, slots_ref, cross_ref, diag_ref, y_ref, tile_ref, hub_ref, sem
):
    s, g = lax.axis_index("sample"), lax.axis_index("gene")
    copy = pltpu.make_async_copy(diag_ref.at[pl.ds(0, 2)], hub_ref, sem)
    copy.start()
    total = jnp.zeros(y_ref.shape, F32)
    for h in range(cross_ref.shape[0]):
        columns = [jnp.where(h == g, 2, column_of(cols_ref, counts_ref, h, p)) for p in range(2)]
        total += dot(slots_ref[h], placed([cross_ref[h, p] for p in range(2)], columns))
    copy.wait()
    total += dot(slots_ref[g], placed([hub_ref[p] for p in range(2)], range(2)))
    y_ref[...] = total.astype(BF)
    for p in range(2):
        tile_ref[p] = jnp.where(s == 0, hub_ref[p], cross_ref[g ^ mask_of(s), p])


def position_of(j):
    back, other = order(ALL)[j]
    s = lax.axis_index("sample")
    chips = lax.axis_size("sample") // 2
    return lax.rem(s // 2 - back + chips, chips) * 2 + (s % 2 ^ other)


def peer_of(j):
    return lax.axis_index("gene") ^ mask_of(position_of(j))


def later_columns_kernel(cols_ref, counts_ref, slots_ref, *refs):
    pieces, y_ref = refs[:-1], refs[-1]
    total = jnp.zeros(y_ref.shape, F32)
    for j, piece in enumerate(pieces):
        h = peer_of(j)
        columns = [column_of(cols_ref, counts_ref, h, p) for p in range(2)]
        total += dot(slots_ref[h], placed([piece[p, :TILE] for p in range(2)], columns))
    y_ref[...] = total.astype(BF)


def gradient_kernel(cols_ref, counts_ref, own_rows_ref, partner_rows_ref, *refs):
    pieces, outs = refs[:-2], refs[-2:]
    g = lax.axis_index("gene")
    for owner, rows_ref, out_ref in zip(owners(), (own_rows_ref, partner_rows_ref), outs):
        total = jnp.zeros((2 * TILE, 2 * TILE), F32)
        for j, piece in enumerate(pieces):
            total += dot_over_rows(rows_ref[j], piece[...])
        for p in range(2):
            rows = total[p * TILE : (p + 1) * TILE]
            column = column_of(cols_ref, counts_ref, g ^ mask_of(owner), p)
            out_ref[p] = jnp.where(column == 1, rows[:, TILE:], rows[:, :TILE])


def proximal(tile, gradient, mirrored, diagonal, sample_total):
    symmetric = 0.5 * (gradient + mirrored.T) / sample_total
    stepped = tile - STEP * symmetric
    shrunk = jnp.where(
        stepped > 0, jnp.maximum(stepped - SHRINK, 0.0), jnp.minimum(stepped + SHRINK, 0.0)
    )
    barrier = 0.5 * (stepped + jnp.sqrt(stepped * stepped + 4.0 * STEP))
    return jnp.where(diagonal, barrier, shrunk)


def eye():
    shape = (TILE, TILE)
    return lax.broadcasted_iota(jnp.int32, shape, 0) == lax.broadcasted_iota(jnp.int32, shape, 1)


def step_kernel(sample_total, cols_ref, counts_ref, tile_ref, *refs):
    (own_ref, partner_ref, mirrored_ref, far_ref), riders = refs[:4], refs[4:-2]
    new_ref, low_ref = refs[-2:]
    s, g = lax.axis_index("sample"), lax.axis_index("gene")
    on_diagonal = jnp.where(s == 0, eye().astype(F32), 0.0) > 0.5
    for p in range(2):
        gradient, mirrored = own_ref[p] + partner_ref[p], mirrored_ref[p] + far_ref[p]
        new = proximal(tile_ref[p], gradient, mirrored, on_diagonal, sample_total)
        new = jnp.where(column_of(cols_ref, counts_ref, g ^ mask_of(s), p) < 2, new, 0.0)
        new_ref[p] = new
        low_ref[p, :TILE] = new.astype(BF)
        for rider in riders:
            low_ref[p, TILE:] = rider[p]


def upper(strict):
    shape = (TILE, TILE)
    row, column = lax.broadcasted_iota(jnp.int32, shape, 0), lax.broadcasted_iota(jnp.int32, shape, 1)
    return row < column if strict else row <= column


def chunk_at(s):
    return (s & 1) * 8 + (s & 2) * 2 + (s & 4) // 2 + (s & 8) // 8


def gram_kernel(x_ref, after_ref, keep_ref, send_ref, all_ref):
    here = chunk_at(lax.axis_index("sample"))
    half = keep_ref.shape[0]
    for b in range(2 * half):
        x = x_ref[:, 2 * b * TILE : 2 * (b + 1) * TILE]
        first, second = (dot_over_rows(x[:, at : at + TILE], x[:, at : at + TILE]) for at in (0, TILE))
        diagonal = jnp.sum(jnp.where(eye(), second, 0.0), axis=0, keepdims=True)
        at = chunk_at(b) ^ here
        all_ref[at, :TILE] = jnp.where(upper(False), first, second)
        all_ref[at, TILE:] = jnp.broadcast_to(diagonal, (EXTRA, TILE))
    keep_ref[...] = all_ref[:half]
    send_ref[...] = all_ref[half:].astype(BF)


def halve_kernel(kept_ref, received_ref, keep_ref, send_ref):
    half = keep_ref.shape[0]
    keep_ref[...] = kept_ref[:half] + received_ref[:half].astype(F32)
    send_ref[...] = (kept_ref[half:] + received_ref[half:].astype(F32)).astype(send_ref.dtype)


def diagonal_kernel(sample_total, kept_ref, received_ref, tiles_ref, out_ref, tile_ref, sem):
    first_tile = 2 * lax.axis_index("sample")
    copy = pltpu.make_async_copy(tiles_ref.at[pl.ds(first_tile, 2)], tile_ref, sem)
    copy.start()
    whole = kept_ref[0] + received_ref[0]
    packed = whole[:TILE]
    turned = packed.T
    first = jnp.where(upper(False), packed, turned)
    second = jnp.where(upper(True), turned, packed)
    second = jnp.where(eye(), whole[TILE : TILE + 1], second)
    copy.wait()
    for p, gram in enumerate((first, second)):
        high = gram.astype(BF)
        low = (gram - high.astype(F32)).astype(BF)
        tile = tile_ref[p]
        for _ in range(ITERS):
            lowered = tile.astype(BF)
            gradient = dot(high, lowered) + dot(low, lowered)
            tile = proximal(tile, gradient, gradient, eye(), sample_total)
        lowered = tile.astype(BF)
        rest = jnp.sum(jnp.where(eye(), tile - lowered.astype(F32), 0.0), axis=0, keepdims=True)
        out_ref[p, :TILE] = lowered
        out_ref[p, TILE:] = jnp.broadcast_to(rest, (EXTRA, TILE)).astype(BF)


def assemble_kernel(*refs):
    pieces, (cross_ref, diag_ref, cross_part, diag_part, cross_sems, diag_sems) = refs[:-6], refs[-6:]
    copies = []
    for j, piece in enumerate(pieces):
        at = position_of(j)
        for p in range(2):
            tile = piece[p, :TILE].astype(F32)
            rest = piece[p, 2 * TILE :].astype(F32)[:1]
            rider = piece[p, TILE : 2 * TILE].astype(F32) + jnp.where(eye(), rest, 0.0)
            cross_part[j, p] = jnp.where(at == 0, 0.0, tile)
            diag_part[j, p] = jnp.where(at == 0, tile, rider)
        copies += [
            pltpu.make_async_copy(cross_part.at[j], cross_ref.at[peer_of(j)], cross_sems.at[j]),
            pltpu.make_async_copy(diag_part.at[j], diag_ref.at[pl.ds(2 * at, 2)], diag_sems.at[j]),
        ]
        for copy in copies[-2:]:
            copy.start()
    for copy in copies:
        copy.wait()


def call(kernel, outs, spaces, *args, scratch=()):
    moved = sum(x.size * x.dtype.itemsize for x in list(args) + jax.tree.leaves(outs))
    return pl.pallas_call(
        kernel,
        out_shape=outs,
        in_specs=list(spaces) + [VMEM] * (len(args) - len(spaces)),
        out_specs=jax.tree.map(lambda _: VMEM, outs),
        compiler_params=PARAMS,
        scratch_shapes=scratch,
        cost_estimate=pl.CostEstimate(flops=10**8, bytes_accessed=moved, transcendentals=0),
    )(*args)


def shards(samples, diag_tiles, cross_tiles, peer_cols, pair_counts):
    s, g = lax.axis_index("sample"), lax.axis_index("gene")
    genes = lax.axis_size("gene")
    rows = samples.shape[0]
    sample_total = rows * lax.axis_size("sample")
    shape = jax.ShapeDtypeStruct
    cols, counts = peer_cols, pair_counts
    part = shape((rows, 2 * TILE), BF)

    hubs = samples[:, : 2 * TILE]
    outgoing = call(outgoing_kernel, shape((genes,) + part.shape, BF), [SMEM], cols, hubs)
    slots = lax.all_to_all(outgoing, "gene", split_axis=0, concat_axis=0, tiled=True)
    rows_shape = shape((len(order(PARITY)),) + part.shape, BF)
    arranged = call(arrange_kernel, [rows_shape] * 2, [SMEM], cols, *gather_shards(hubs, PARITY))
    own_rows = swap_owner(arranged[0], 0, lambda s: MASKS[s])
    partner_rows = swap_owner(arranged[1], 0, lambda s: MASKS[s ^ PARTNER])

    pair = (2, TILE, TILE)
    for iteration in range(ITERS):
        if iteration == 0:
            columns, tile = call(
                first_columns_kernel,
                [part, shape(pair, F32)],
                [SMEM, SMEM, VMEM, VMEM, ANY],
                cols, counts, slots, cross_tiles[0], diag_tiles,
                scratch=[pltpu.VMEM(pair, F32), pltpu.SemaphoreType.DMA(())],
            )
            chunk = (TILE + EXTRA, TILE)
            count = diag_tiles.shape[0] // 2
            kept, sent = call(
                gram_kernel,
                [shape((count // 2,) + chunk, F32), shape((count // 2,) + chunk, BF)],
                [VMEM, ANY],
                samples, columns,
                scratch=[pltpu.VMEM((count,) + chunk, F32)],
            )
            received = swap_core(sent)
            for bit, dtype in ((2, BF), (4, F32), (8, F32)):
                half = (kept.shape[0] // 2,) + chunk
                kept, sent = call(halve_kernel, [shape(half, F32), shape(half, dtype)], [], kept, received)
                received = lax.ppermute(sent, "sample", [(i, i ^ bit) for i in range(lax.axis_size("sample"))])
            my_diag = call(
                functools.partial(diagonal_kernel, sample_total),
                shape((2,) + chunk, BF),
                [VMEM, VMEM, ANY],
                kept, received, diag_tiles,
                scratch=[pltpu.VMEM((2, TILE, TILE), F32), pltpu.SemaphoreType.DMA(())],
            )
        else:
            columns = call(later_columns_kernel, part, [SMEM, SMEM], cols, counts, slots, *pieces)
        own, partner = call(
            gradient_kernel,
            [shape(pair, F32)] * 2,
            [SMEM, SMEM],
            cols, counts, own_rows, partner_rows, *gather_shards(columns, PARITY),
        )
        others = (
            swap_owner(partner, PARTNER, lambda s: 0),
            swap_owner(own, 0, lambda s: MASKS[s]),
            swap_owner(partner, PARTNER, lambda s: MASKS[s ^ PARTNER]),
        )
        riders = [my_diag] if iteration == ITERS - 1 else []
        tile, lowered = call(
            functools.partial(step_kernel, sample_total),
            [shape(pair, F32), shape((2, TILE + sum(r.shape[1] for r in riders), TILE), BF)],
            [SMEM, SMEM],
            cols, counts, tile, own, *others, *riders,
        )
        pieces = forward_shards(lowered) if riders else gather_shards(lowered, ALL)

    place = pl.BlockSpec(memory_space=pl.ANY)
    chunk = pltpu.VMEM((len(pieces),) + pair, F32)
    cross, diag = pl.pallas_call(
        assemble_kernel,
        out_shape=[shape(cross_tiles.shape[1:], F32), shape(diag_tiles.shape, F32)],
        in_specs=[VMEM] * len(pieces),
        out_specs=[place, place],
        scratch_shapes=[chunk, chunk] + [pltpu.SemaphoreType.DMA((len(pieces),))] * 2,
        compiler_params=PARAMS,
    )(*pieces)
    return diag, cross[None]


def solution(mesh):
    in_specs = (
        P("sample", "gene"),
        P("gene", None, None),
        P("gene", None, None, None, None),
        P("gene", None, None),
        P("gene", None),
    )
    out_specs = (P("gene", None, None), P("gene", None, None, None, None))
    return jax.shard_map(shards, mesh=mesh, in_specs=in_specs, out_specs=out_specs, check_vma=False)
```

```python
import functools

import jax
import jax.numpy as jnp
from jax import lax
from jax.experimental import pallas as pl
from jax.experimental.pallas import tpu as pltpu
from jax.sharding import PartitionSpec as P

ITERS = 2
STEP = 0.5
SHRINK = 0.02
TILE = 128
EXTRA = 16
BF = jnp.bfloat16
F32 = jnp.float32

ALL = (0, 1, -1, 2, -2, 3, -3, 4)
PARITY = (0, 2, -2, 4)
MASKS = tuple(
    4 * y + x
    for (x, y) in (
        (0, 0), (2, 2), (2, 0), (0, 2), (2, 1), (0, 3), (2, 3), (0, 1),
        (1, 0), (3, 2), (3, 0), (1, 2), (1, 1), (3, 3), (1, 3), (3, 1),
    )
)
PARTNER = 2


def order(backs):
    return tuple((back, other) for other in (0, 1) for back in backs)


VMEM = pl.BlockSpec(memory_space=pltpu.VMEM)
SMEM = pl.BlockSpec(memory_space=pltpu.SMEM)
ANY = pl.BlockSpec(memory_space=pl.ANY)
PARAMS = pltpu.CompilerParams(vmem_limit_bytes=16 * 1024 * 1024)


def shift_z(x, chips):
    count = lax.axis_size("sample")
    return lax.ppermute(x, "sample", [(i, (i + 2 * chips) % count) for i in range(count)])


def swap_core(x):
    count = lax.axis_size("sample")
    return lax.ppermute(x, "sample", [(i, i ^ 1) for i in range(count)])


def gather_shards(x, backs):
    own = [x] + [shift_z(x, back) for back in backs[1:]]
    return own + [swap_core(piece) for piece in own]


def forward_shards(x):
    up, down, up2, down2 = (shift_z(x, back) for back in (1, -1, 2, -2))
    half = x.shape[0] // 2
    far = jnp.concatenate([shift_z(up2[:half], 2), shift_z(down2[half:], -2)], axis=0)
    own = [x, up, down, up2, down2, shift_z(up2, 1), shift_z(down2, -1), far]
    return own + [swap_core(piece) for piece in own]


def swap_owner(x, sample_xor, gene_xor):
    samples, genes = lax.axis_size("sample"), lax.axis_size("gene")
    pairs = [
        (s * genes + g, (s ^ sample_xor) * genes + (g ^ gene_xor(s)))
        for s in range(samples)
        for g in range(genes)
    ]
    return lax.ppermute(x, ("sample", "gene"), pairs)


def dot(a, b):
    return jnp.dot(a, b, preferred_element_type=F32)


def dot_over_rows(a, b):
    return lax.dot_general(a, b, (((0,), (0,)), ((), ())), preferred_element_type=F32)


def column_of(cols_ref, counts_ref, h, p):
    live = jnp.where(p < counts_ref[0, h], cols_ref[0, h, p], 2)
    return jnp.where(h == lax.axis_index("gene"), p, live)


def pick_blocks(cols_ref, h, own, left, right):
    picks = [jnp.where(own, p, cols_ref[0, h, p]) for p in range(2)]
    return jnp.concatenate([jnp.where(pick == 1, right, left) for pick in picks], axis=-1)


def outgoing_kernel(cols_ref, x_ref, out_ref):
    left, right = x_ref[:, :TILE], x_ref[:, TILE:]
    for h in range(out_ref.shape[0]):
        out_ref[h] = pick_blocks(cols_ref, h, h == lax.axis_index("gene"), left, right)


def arrange_kernel(cols_ref, *refs):
    pieces, outs = refs[:-2], refs[-2:]
    g = lax.axis_index("gene")
    for owner, out_ref in zip(owners(), outs):
        for j, piece in enumerate(pieces):
            out_ref[j] = pick_blocks(cols_ref, g ^ mask_of(owner), owner == 0, piece[:, :TILE], piece[:, TILE:])


def mask_of(s):
    mask = s * 0
    for at, value in enumerate(MASKS):
        mask = jnp.where(s == at, value, mask)
    return mask


def owners():
    s = lax.axis_index("sample")
    return s, s ^ PARTNER


def placed(tiles, columns):
    zero = jnp.zeros((TILE, TILE), BF)
    rows = [
        jnp.concatenate([jnp.where(column == c, tile.astype(BF), zero) for c in range(2)], axis=1)
        for tile, column in zip(tiles, columns)
    ]
    return jnp.concatenate(rows, axis=0)


def first_columns_kernel(
    cols_ref, counts_ref, slots_ref, cross_ref, diag_ref, y_ref, tile_ref, hub_ref, sem
):
    s, g = lax.axis_index("sample"), lax.axis_index("gene")
    copy = pltpu.make_async_copy(diag_ref.at[pl.ds(0, 2)], hub_ref, sem)
    copy.start()
    total = jnp.zeros(y_ref.shape, F32)
    for h in range(cross_ref.shape[0]):
        columns = [jnp.where(h == g, 2, column_of(cols_ref, counts_ref, h, p)) for p in range(2)]
        total += dot(slots_ref[h], placed([cross_ref[h, p] for p in range(2)], columns))
    copy.wait()
    total += dot(slots_ref[g], placed([hub_ref[p] for p in range(2)], range(2)))
    y_ref[...] = total.astype(BF)
    for p in range(2):
        tile_ref[p] = jnp.where(s == 0, hub_ref[p], cross_ref[g ^ mask_of(s), p])


def position_of(j):
    back, other = order(ALL)[j]
    s = lax.axis_index("sample")
    chips = lax.axis_size("sample") // 2
    return lax.rem(s // 2 - back + chips, chips) * 2 + (s % 2 ^ other)


def peer_of(j):
    return lax.axis_index("gene") ^ mask_of(position_of(j))


def later_columns_kernel(cols_ref, counts_ref, after_ref, slots_ref, *refs):
    pieces, y_ref = refs[:-1], refs[-1]
    total = jnp.zeros(y_ref.shape, F32)
    for j, piece in enumerate(pieces):
        h = peer_of(j)
        columns = [column_of(cols_ref, counts_ref, h, p) for p in range(2)]
        total += dot(slots_ref[h], placed([piece[p, :TILE] for p in range(2)], columns))
    y_ref[...] = total.astype(BF)


def gradient_kernel(cols_ref, counts_ref, own_rows_ref, partner_rows_ref, *refs):
    pieces, outs = refs[:-2], refs[-2:]
    g = lax.axis_index("gene")
    for owner, rows_ref, out_ref in zip(owners(), (own_rows_ref, partner_rows_ref), outs):
        total = jnp.zeros((2 * TILE, 2 * TILE), F32)
        for j, piece in enumerate(pieces):
            total += dot_over_rows(rows_ref[j], piece[...])
        for p in range(2):
            rows = total[p * TILE : (p + 1) * TILE]
            column = column_of(cols_ref, counts_ref, g ^ mask_of(owner), p)
            out_ref[p] = jnp.where(column == 1, rows[:, TILE:], rows[:, :TILE])


def proximal(tile, gradient, mirrored, diagonal, sample_total):
    symmetric = 0.5 * (gradient + mirrored.T) / sample_total
    stepped = tile - STEP * symmetric
    shrunk = jnp.where(
        stepped > 0, jnp.maximum(stepped - SHRINK, 0.0), jnp.minimum(stepped + SHRINK, 0.0)
    )
    barrier = 0.5 * (stepped + jnp.sqrt(stepped * stepped + 4.0 * STEP))
    return jnp.where(diagonal, barrier, shrunk)


def eye():
    shape = (TILE, TILE)
    return lax.broadcasted_iota(jnp.int32, shape, 0) == lax.broadcasted_iota(jnp.int32, shape, 1)


def step_kernel(sample_total, cols_ref, counts_ref, tile_ref, *refs):
    (own_ref, partner_ref, mirrored_ref, far_ref), riders = refs[:4], refs[4:-2]
    new_ref, low_ref = refs[-2:]
    s, g = lax.axis_index("sample"), lax.axis_index("gene")
    on_diagonal = jnp.where(s == 0, eye().astype(F32), 0.0) > 0.5
    for p in range(2):
        gradient, mirrored = own_ref[p] + partner_ref[p], mirrored_ref[p] + far_ref[p]
        new = proximal(tile_ref[p], gradient, mirrored, on_diagonal, sample_total)
        new = jnp.where(column_of(cols_ref, counts_ref, g ^ mask_of(s), p) < 2, new, 0.0)
        new_ref[p] = new
        low_ref[p, :TILE] = new.astype(BF)
        for rider in riders:
            low_ref[p, TILE:] = rider[p]


def upper(strict):
    shape = (TILE, TILE)
    row, column = lax.broadcasted_iota(jnp.int32, shape, 0), lax.broadcasted_iota(jnp.int32, shape, 1)
    return row < column if strict else row <= column


def chunk_at(s):
    return (s & 1) * 8 + (s & 2) * 2 + (s & 4) // 2 + (s & 8) // 8


def gram_kernel(x_ref, after_ref, keep_ref, send_ref, all_ref):
    here = chunk_at(lax.axis_index("sample"))
    half = keep_ref.shape[0]
    for b in range(2 * half):
        x = x_ref[:, 2 * b * TILE : 2 * (b + 1) * TILE]
        first, second = (dot_over_rows(x[:, at : at + TILE], x[:, at : at + TILE]) for at in (0, TILE))
        diagonal = jnp.sum(jnp.where(eye(), second, 0.0), axis=0, keepdims=True)
        at = chunk_at(b) ^ here
        all_ref[at, :TILE] = jnp.where(upper(False), first, second)
        all_ref[at, TILE:] = jnp.broadcast_to(diagonal, (EXTRA, TILE))
    keep_ref[...] = all_ref[:half]
    send_ref[...] = all_ref[half:].astype(BF)


def halve_kernel(kept_ref, received_ref, keep_ref, send_ref):
    half = keep_ref.shape[0]
    keep_ref[...] = kept_ref[:half] + received_ref[:half].astype(F32)
    send_ref[...] = (kept_ref[half:] + received_ref[half:].astype(F32)).astype(send_ref.dtype)


def diagonal_kernel(sample_total, kept_ref, received_ref, tiles_ref, out_ref, tile_ref, sem):
    first_tile = 2 * lax.axis_index("sample")
    copy = pltpu.make_async_copy(tiles_ref.at[pl.ds(first_tile, 2)], tile_ref, sem)
    copy.start()
    whole = kept_ref[0] + received_ref[0]
    packed = whole[:TILE]
    turned = packed.T
    first = jnp.where(upper(False), packed, turned)
    second = jnp.where(upper(True), turned, packed)
    second = jnp.where(eye(), whole[TILE : TILE + 1], second)
    copy.wait()
    for p, gram in enumerate((first, second)):
        high = gram.astype(BF)
        low = (gram - high.astype(F32)).astype(BF)
        tile = tile_ref[p]
        for _ in range(ITERS):
            lowered = tile.astype(BF)
            gradient = dot(high, lowered) + dot(low, lowered)
            tile = proximal(tile, gradient, gradient, eye(), sample_total)
        lowered = tile.astype(BF)
        rest = jnp.sum(jnp.where(eye(), tile - lowered.astype(F32), 0.0), axis=0, keepdims=True)
        out_ref[p, :TILE] = lowered
        out_ref[p, TILE:] = jnp.broadcast_to(rest, (EXTRA, TILE)).astype(BF)


def assemble_kernel(*refs):
    pieces, (cross_ref, diag_ref, cross_part, diag_part, cross_sems, diag_sems) = refs[:-6], refs[-6:]
    copies = []
    for j, piece in enumerate(pieces):
        at = position_of(j)
        for p in range(2):
            tile = piece[p, :TILE].astype(F32)
            rest = piece[p, 2 * TILE :].astype(F32)[:1]
            rider = piece[p, TILE : 2 * TILE].astype(F32) + jnp.where(eye(), rest, 0.0)
            cross_part[j, p] = jnp.where(at == 0, 0.0, tile)
            diag_part[j, p] = jnp.where(at == 0, tile, rider)
        copies += [
            pltpu.make_async_copy(cross_part.at[j], cross_ref.at[peer_of(j)], cross_sems.at[j]),
            pltpu.make_async_copy(diag_part.at[j], diag_ref.at[pl.ds(2 * at, 2)], diag_sems.at[j]),
        ]
        for copy in copies[-2:]:
            copy.start()
    for copy in copies:
        copy.wait()


def call(kernel, outs, spaces, *args, scratch=()):
    moved = sum(x.size * x.dtype.itemsize for x in list(args) + jax.tree.leaves(outs))
    return pl.pallas_call(
        kernel,
        out_shape=outs,
        in_specs=list(spaces) + [VMEM] * (len(args) - len(spaces)),
        out_specs=jax.tree.map(lambda _: VMEM, outs),
        compiler_params=PARAMS,
        scratch_shapes=scratch,
        cost_estimate=pl.CostEstimate(flops=10**8, bytes_accessed=moved, transcendentals=0),
    )(*args)


def shards(samples, diag_tiles, cross_tiles, peer_cols, pair_counts):
    s, g = lax.axis_index("sample"), lax.axis_index("gene")
    genes = lax.axis_size("gene")
    rows = samples.shape[0]
    sample_total = rows * lax.axis_size("sample")
    shape = jax.ShapeDtypeStruct
    cols, counts = peer_cols, pair_counts
    part = shape((rows, 2 * TILE), BF)

    hubs = samples[:, : 2 * TILE]
    outgoing = call(outgoing_kernel, shape((genes,) + part.shape, BF), [SMEM], cols, hubs)
    slots = lax.all_to_all(outgoing, "gene", split_axis=0, concat_axis=0, tiled=True)
    rows_shape = shape((len(order(PARITY)),) + part.shape, BF)
    arranged = call(arrange_kernel, [rows_shape] * 2, [SMEM], cols, *gather_shards(hubs, PARITY))
    own_rows = swap_owner(arranged[0], 0, lambda s: MASKS[s])
    partner_rows = swap_owner(arranged[1], 0, lambda s: MASKS[s ^ PARTNER])

    pair = (2, TILE, TILE)
    for iteration in range(ITERS):
        if iteration == 0:
            columns, tile = call(
                first_columns_kernel,
                [part, shape(pair, F32)],
                [SMEM, SMEM, VMEM, VMEM, ANY],
                cols, counts, slots, cross_tiles[0], diag_tiles,
                scratch=[pltpu.VMEM(pair, F32), pltpu.SemaphoreType.DMA(())],
            )
            chunk = (TILE + EXTRA, TILE)
            count = diag_tiles.shape[0] // 2
            kept, sent = call(
                gram_kernel,
                [shape((count // 2,) + chunk, F32), shape((count // 2,) + chunk, BF)],
                [VMEM, ANY],
                samples, columns,
                scratch=[pltpu.VMEM((count,) + chunk, F32)],
            )
            received = swap_core(sent)
            for bit, dtype in ((2, BF), (4, F32), (8, F32)):
                half = (kept.shape[0] // 2,) + chunk
                kept, sent = call(halve_kernel, [shape(half, F32), shape(half, dtype)], [], kept, received)
                received = lax.ppermute(sent, "sample", [(i, i ^ bit) for i in range(lax.axis_size("sample"))])
            my_diag = call(
                functools.partial(diagonal_kernel, sample_total),
                shape((2,) + chunk, BF),
                [VMEM, VMEM, ANY],
                kept, received, diag_tiles,
                scratch=[pltpu.VMEM((2, TILE, TILE), F32), pltpu.SemaphoreType.DMA(())],
            )
        else:
            columns = call(
                later_columns_kernel, part, [SMEM, SMEM, ANY], cols, counts, my_diag, slots, *pieces
            )
        own, partner = call(
            gradient_kernel,
            [shape(pair, F32)] * 2,
            [SMEM, SMEM],
            cols, counts, own_rows, partner_rows, *gather_shards(columns, PARITY),
        )
        others = (
            swap_owner(partner, PARTNER, lambda s: 0),
            swap_owner(own, 0, lambda s: MASKS[s]),
            swap_owner(partner, PARTNER, lambda s: MASKS[s ^ PARTNER]),
        )
        riders = [my_diag] if iteration == ITERS - 1 else []
        tile, lowered = call(
            functools.partial(step_kernel, sample_total),
            [shape(pair, F32), shape((2, TILE + sum(r.shape[1] for r in riders), TILE), BF)],
            [SMEM, SMEM],
            cols, counts, tile, own, *others, *riders,
        )
        pieces = forward_shards(lowered) if riders else gather_shards(lowered, ALL)

    place = pl.BlockSpec(memory_space=pl.ANY)
    chunk = pltpu.VMEM((len(pieces),) + pair, F32)
    cross, diag = pl.pallas_call(
        assemble_kernel,
        out_shape=[shape(cross_tiles.shape[1:], F32), shape(diag_tiles.shape, F32)],
        in_specs=[VMEM] * len(pieces),
        out_specs=[place, place],
        scratch_shapes=[chunk, chunk] + [pltpu.SemaphoreType.DMA((len(pieces),))] * 2,
        compiler_params=PARAMS,
    )(*pieces)
    return diag, cross[None]


def solution(mesh):
    in_specs = (
        P("sample", "gene"),
        P("gene", None, None),
        P("gene", None, None, None, None),
        P("gene", None, None),
        P("gene", None),
    )
    out_specs = (P("gene", None, None), P("gene", None, None, None, None))
    return jax.shard_map(shards, mesh=mesh, in_specs=in_specs, out_specs=out_specs, check_vma=False)
```

```python
import functools

import jax
import jax.numpy as jnp
from jax import lax
from jax.experimental import pallas as pl
from jax.experimental.pallas import tpu as pltpu
from jax.sharding import PartitionSpec as P

ITERS = 2
STEP = 0.5
SHRINK = 0.02
TILE = 128
EXTRA = 16
BF = jnp.bfloat16
F32 = jnp.float32

ALL = (0, 1, -1, 2, -2, 3, -3, 4)
PARITY = (0, 2, -2, 4)
MASKS = tuple(
    4 * y + x
    for (x, y) in (
        (0, 0), (2, 2), (2, 0), (0, 2), (2, 1), (0, 3), (2, 3), (0, 1),
        (1, 0), (3, 2), (3, 0), (1, 2), (1, 1), (3, 3), (1, 3), (3, 1),
    )
)
PARTNER = 2


def order(backs):
    return tuple((back, other) for other in (0, 1) for back in backs)


VMEM = pl.BlockSpec(memory_space=pltpu.VMEM)
SMEM = pl.BlockSpec(memory_space=pltpu.SMEM)
ANY = pl.BlockSpec(memory_space=pl.ANY)
HBM = pl.BlockSpec(memory_space=pltpu.HBM)
PARAMS = pltpu.CompilerParams(vmem_limit_bytes=16 * 1024 * 1024)


def shift_z(x, chips):
    count = lax.axis_size("sample")
    return lax.ppermute(x, "sample", [(i, (i + 2 * chips) % count) for i in range(count)])


def swap_core(x):
    count = lax.axis_size("sample")
    return lax.ppermute(x, "sample", [(i, i ^ 1) for i in range(count)])


def gather_shards(x, backs):
    own = [x] + [shift_z(x, back) for back in backs[1:]]
    return own + [swap_core(piece) for piece in own]


def forward_shards(x):
    up, down, up2, down2 = (shift_z(x, back) for back in (1, -1, 2, -2))
    half = x.shape[0] // 2
    far = jnp.concatenate([shift_z(up2[:half], 2), shift_z(down2[half:], -2)], axis=0)
    own = [x, up, down, up2, down2, shift_z(up2, 1), shift_z(down2, -1), far]
    return own + [swap_core(piece) for piece in own]


def swap_owner(x, sample_xor, gene_xor):
    samples, genes = lax.axis_size("sample"), lax.axis_size("gene")
    pairs = [
        (s * genes + g, (s ^ sample_xor) * genes + (g ^ gene_xor(s)))
        for s in range(samples)
        for g in range(genes)
    ]
    return lax.ppermute(x, ("sample", "gene"), pairs)


def dot(a, b):
    return jnp.dot(a, b, preferred_element_type=F32)


def dot_over_rows(a, b):
    return lax.dot_general(a, b, (((0,), (0,)), ((), ())), preferred_element_type=F32)


def column_of(cols_ref, counts_ref, h, p):
    live = jnp.where(p < counts_ref[0, h], cols_ref[0, h, p], 2)
    return jnp.where(h == lax.axis_index("gene"), p, live)


def pick_blocks(cols_ref, h, own, left, right):
    picks = [jnp.where(own, p, cols_ref[0, h, p]) for p in range(2)]
    return jnp.concatenate([jnp.where(pick == 1, right, left) for pick in picks], axis=-1)


def outgoing_kernel(cols_ref, x_ref, out_ref):
    left, right = x_ref[:, :TILE], x_ref[:, TILE:]
    for h in range(out_ref.shape[0]):
        out_ref[h] = pick_blocks(cols_ref, h, h == lax.axis_index("gene"), left, right)


def arrange_kernel(cols_ref, *refs):
    pieces, outs = refs[:-2], refs[-2:]
    g = lax.axis_index("gene")
    for owner, out_ref in zip(owners(), outs):
        for j, piece in enumerate(pieces):
            out_ref[j] = pick_blocks(cols_ref, g ^ mask_of(owner), owner == 0, piece[:, :TILE], piece[:, TILE:])


def mask_of(s):
    mask = s * 0
    for at, value in enumerate(MASKS):
        mask = jnp.where(s == at, value, mask)
    return mask


def owners():
    s = lax.axis_index("sample")
    return s, s ^ PARTNER


def placed(tiles, columns):
    zero = jnp.zeros((TILE, TILE), BF)
    rows = [
        jnp.concatenate([jnp.where(column == c, tile.astype(BF), zero) for c in range(2)], axis=1)
        for tile, column in zip(tiles, columns)
    ]
    return jnp.concatenate(rows, axis=0)


def first_columns_kernel(
    cols_ref, counts_ref, slots_ref, cross_ref, diag_ref, y_ref, tile_ref, hub_ref, sem
):
    s, g = lax.axis_index("sample"), lax.axis_index("gene")
    copy = pltpu.make_async_copy(diag_ref.at[pl.ds(0, 2)], hub_ref, sem)
    copy.start()
    total = jnp.zeros(y_ref.shape, F32)
    for h in range(cross_ref.shape[0]):
        columns = [jnp.where(h == g, 2, column_of(cols_ref, counts_ref, h, p)) for p in range(2)]
        total += dot(slots_ref[h], placed([cross_ref[h, p] for p in range(2)], columns))
    copy.wait()
    total += dot(slots_ref[g], placed([hub_ref[p] for p in range(2)], range(2)))
    y_ref[...] = total.astype(BF)
    for p in range(2):
        tile_ref[p] = jnp.where(s == 0, hub_ref[p], cross_ref[g ^ mask_of(s), p])


def position_of(j):
    back, other = order(ALL)[j]
    s = lax.axis_index("sample")
    chips = lax.axis_size("sample") // 2
    return lax.rem(s // 2 - back + chips, chips) * 2 + (s % 2 ^ other)


def peer_of(j):
    return lax.axis_index("gene") ^ mask_of(position_of(j))


def later_columns_kernel(cols_ref, counts_ref, slots_ref, *refs):
    pieces, y_ref = refs[:-1], refs[-1]
    total = jnp.zeros(y_ref.shape, F32)
    for j, piece in enumerate(pieces):
        h = peer_of(j)
        columns = [column_of(cols_ref, counts_ref, h, p) for p in range(2)]
        total += dot(slots_ref[h], placed([piece[p, :TILE] for p in range(2)], columns))
    y_ref[...] = total.astype(BF)


def gradient_kernel(cols_ref, counts_ref, own_rows_ref, partner_rows_ref, *refs):
    pieces, outs = refs[:-2], refs[-2:]
    g = lax.axis_index("gene")
    for owner, rows_ref, out_ref in zip(owners(), (own_rows_ref, partner_rows_ref), outs):
        total = jnp.zeros((2 * TILE, 2 * TILE), F32)
        for j, piece in enumerate(pieces):
            total += dot_over_rows(rows_ref[j], piece[...])
        for p in range(2):
            rows = total[p * TILE : (p + 1) * TILE]
            column = column_of(cols_ref, counts_ref, g ^ mask_of(owner), p)
            out_ref[p] = jnp.where(column == 1, rows[:, TILE:], rows[:, :TILE])


def proximal(tile, gradient, mirrored, diagonal, sample_total):
    symmetric = 0.5 * (gradient + mirrored.T) / sample_total
    stepped = tile - STEP * symmetric
    shrunk = jnp.where(
        stepped > 0, jnp.maximum(stepped - SHRINK, 0.0), jnp.minimum(stepped + SHRINK, 0.0)
    )
    barrier = 0.5 * (stepped + jnp.sqrt(stepped * stepped + 4.0 * STEP))
    return jnp.where(diagonal, barrier, shrunk)


def eye():
    shape = (TILE, TILE)
    return lax.broadcasted_iota(jnp.int32, shape, 0) == lax.broadcasted_iota(jnp.int32, shape, 1)


def step_kernel(sample_total, cols_ref, counts_ref, tile_ref, *refs):
    (own_ref, partner_ref, mirrored_ref, far_ref), riders = refs[:4], refs[4:-2]
    new_ref, low_ref = refs[-2:]
    s, g = lax.axis_index("sample"), lax.axis_index("gene")
    on_diagonal = jnp.where(s == 0, eye().astype(F32), 0.0) > 0.5
    for p in range(2):
        gradient, mirrored = own_ref[p] + partner_ref[p], mirrored_ref[p] + far_ref[p]
        new = proximal(tile_ref[p], gradient, mirrored, on_diagonal, sample_total)
        new = jnp.where(column_of(cols_ref, counts_ref, g ^ mask_of(s), p) < 2, new, 0.0)
        new_ref[p] = new
        low_ref[p, :TILE] = new.astype(BF)
        for rider in riders:
            low_ref[p, TILE:] = rider[p]


def upper(strict):
    shape = (TILE, TILE)
    row, column = lax.broadcasted_iota(jnp.int32, shape, 0), lax.broadcasted_iota(jnp.int32, shape, 1)
    return row < column if strict else row <= column


def chunk_at(s):
    return (s & 1) * 8 + (s & 2) * 2 + (s & 4) // 2 + (s & 8) // 8


def gram_kernel(x_ref, after_ref, keep_ref, send_ref, all_ref):
    here = chunk_at(lax.axis_index("sample"))
    half = keep_ref.shape[0]
    for b in range(2 * half):
        x = x_ref[:, 2 * b * TILE : 2 * (b + 1) * TILE]
        first, second = (dot_over_rows(x[:, at : at + TILE], x[:, at : at + TILE]) for at in (0, TILE))
        diagonal = jnp.sum(jnp.where(eye(), second, 0.0), axis=0, keepdims=True)
        at = chunk_at(b) ^ here
        all_ref[at, :TILE] = jnp.where(upper(False), first, second)
        all_ref[at, TILE:] = jnp.broadcast_to(diagonal, (EXTRA, TILE))
    keep_ref[...] = all_ref[:half]
    send_ref[...] = all_ref[half:].astype(BF)


def halve_kernel(kept_ref, received_ref, keep_ref, send_ref):
    half = keep_ref.shape[0]
    keep_ref[...] = kept_ref[:half] + received_ref[:half].astype(F32)
    send_ref[...] = (kept_ref[half:] + received_ref[half:].astype(F32)).astype(send_ref.dtype)


def diagonal_kernel(sample_total, kept_ref, received_ref, tiles_ref, out_ref, tile_ref, sem):
    first_tile = 2 * lax.axis_index("sample")
    copy = pltpu.make_async_copy(tiles_ref.at[pl.ds(first_tile, 2)], tile_ref, sem)
    copy.start()
    whole = kept_ref[0] + received_ref[0]
    packed = whole[:TILE]
    turned = packed.T
    first = jnp.where(upper(False), packed, turned)
    second = jnp.where(upper(True), turned, packed)
    second = jnp.where(eye(), whole[TILE : TILE + 1], second)
    copy.wait()
    for p, gram in enumerate((first, second)):
        high = gram.astype(BF)
        low = (gram - high.astype(F32)).astype(BF)
        tile = tile_ref[p]
        for _ in range(ITERS):
            lowered = tile.astype(BF)
            gradient = dot(high, lowered) + dot(low, lowered)
            tile = proximal(tile, gradient, gradient, eye(), sample_total)
        lowered = tile.astype(BF)
        rest = jnp.sum(jnp.where(eye(), tile - lowered.astype(F32), 0.0), axis=0, keepdims=True)
        out_ref[p, :TILE] = lowered
        out_ref[p, TILE:] = jnp.broadcast_to(rest, (EXTRA, TILE)).astype(BF)


def assemble_kernel(*refs):
    pieces, (cross_ref, diag_ref, cross_part, diag_part, cross_sems, diag_sems) = refs[:-6], refs[-6:]
    copies = []
    for j, piece in enumerate(pieces):
        at = position_of(j)
        for p in range(2):
            tile = piece[p, :TILE].astype(F32)
            rest = piece[p, 2 * TILE :].astype(F32)[:1]
            rider = piece[p, TILE : 2 * TILE].astype(F32) + jnp.where(eye(), rest, 0.0)
            cross_part[j, p] = jnp.where(at == 0, 0.0, tile)
            diag_part[j, p] = jnp.where(at == 0, tile, rider)
        copies += [
            pltpu.make_async_copy(cross_part.at[j], cross_ref.at[peer_of(j)], cross_sems.at[j]),
            pltpu.make_async_copy(diag_part.at[j], diag_ref.at[pl.ds(2 * at, 2)], diag_sems.at[j]),
        ]
        for copy in copies[-2:]:
            copy.start()
    for copy in copies:
        copy.wait()


def call(kernel, outs, spaces, *args, scratch=()):
    moved = sum(x.size * x.dtype.itemsize for x in list(args) + jax.tree.leaves(outs))
    return pl.pallas_call(
        kernel,
        out_shape=outs,
        in_specs=list(spaces) + [VMEM] * (len(args) - len(spaces)),
        out_specs=jax.tree.map(lambda _: VMEM, outs),
        compiler_params=PARAMS,
        scratch_shapes=scratch,
        cost_estimate=pl.CostEstimate(flops=10**8, bytes_accessed=moved, transcendentals=0),
    )(*args)


def shards(samples, diag_tiles, cross_tiles, peer_cols, pair_counts):
    s, g = lax.axis_index("sample"), lax.axis_index("gene")
    genes = lax.axis_size("gene")
    rows = samples.shape[0]
    sample_total = rows * lax.axis_size("sample")
    shape = jax.ShapeDtypeStruct
    cols, counts = peer_cols, pair_counts
    part = shape((rows, 2 * TILE), BF)

    hubs = samples[:, : 2 * TILE]
    outgoing = call(outgoing_kernel, shape((genes,) + part.shape, BF), [SMEM], cols, hubs)
    slots = lax.all_to_all(outgoing, "gene", split_axis=0, concat_axis=0, tiled=True)
    rows_shape = shape((len(order(PARITY)),) + part.shape, BF)
    arranged = call(arrange_kernel, [rows_shape] * 2, [SMEM], cols, *gather_shards(hubs, PARITY))
    own_rows = swap_owner(arranged[0], 0, lambda s: MASKS[s])
    partner_rows = swap_owner(arranged[1], 0, lambda s: MASKS[s ^ PARTNER])

    pair = (2, TILE, TILE)
    for iteration in range(ITERS):
        if iteration == 0:
            columns, tile = call(
                first_columns_kernel,
                [part, shape(pair, F32)],
                [SMEM, SMEM, VMEM, VMEM, HBM],
                cols, counts, slots, cross_tiles[0], diag_tiles,
                scratch=[pltpu.VMEM(pair, F32), pltpu.SemaphoreType.DMA(())],
            )
            chunk = (TILE + EXTRA, TILE)
            count = diag_tiles.shape[0] // 2
            kept, sent = call(
                gram_kernel,
                [shape((count // 2,) + chunk, F32), shape((count // 2,) + chunk, BF)],
                [VMEM, ANY],
                samples, columns,
                scratch=[pltpu.VMEM((count,) + chunk, F32)],
            )
            received = swap_core(sent)
            for bit, dtype in ((2, BF), (4, F32), (8, F32)):
                half = (kept.shape[0] // 2,) + chunk
                kept, sent = call(halve_kernel, [shape(half, F32), shape(half, dtype)], [], kept, received)
                received = lax.ppermute(sent, "sample", [(i, i ^ bit) for i in range(lax.axis_size("sample"))])
            my_diag = call(
                functools.partial(diagonal_kernel, sample_total),
                shape((2,) + chunk, BF),
                [VMEM, VMEM, HBM],
                kept, received, diag_tiles,
                scratch=[pltpu.VMEM((2, TILE, TILE), F32), pltpu.SemaphoreType.DMA(())],
            )
        else:
            columns = call(later_columns_kernel, part, [SMEM, SMEM], cols, counts, slots, *pieces)
        own, partner = call(
            gradient_kernel,
            [shape(pair, F32)] * 2,
            [SMEM, SMEM],
            cols, counts, own_rows, partner_rows, *gather_shards(columns, PARITY),
        )
        others = (
            swap_owner(partner, PARTNER, lambda s: 0),
            swap_owner(own, 0, lambda s: MASKS[s]),
            swap_owner(partner, PARTNER, lambda s: MASKS[s ^ PARTNER]),
        )
        riders = [my_diag] if iteration == ITERS - 1 else []
        tile, lowered = call(
            functools.partial(step_kernel, sample_total),
            [shape(pair, F32), shape((2, TILE + sum(r.shape[1] for r in riders), TILE), BF)],
            [SMEM, SMEM],
            cols, counts, tile, own, *others, *riders,
        )
        pieces = forward_shards(lowered) if riders else gather_shards(lowered, ALL)

    place = pl.BlockSpec(memory_space=pl.ANY)
    chunk = pltpu.VMEM((len(pieces),) + pair, F32)
    cross, diag = pl.pallas_call(
        assemble_kernel,
        out_shape=[shape(cross_tiles.shape[1:], F32), shape(diag_tiles.shape, F32)],
        in_specs=[VMEM] * len(pieces),
        out_specs=[place, place],
        scratch_shapes=[chunk, chunk] + [pltpu.SemaphoreType.DMA((len(pieces),))] * 2,
        compiler_params=PARAMS,
    )(*pieces)
    return diag, cross[None]


def solution(mesh):
    in_specs = (
        P("sample", "gene"),
        P("gene", None, None),
        P("gene", None, None, None, None),
        P("gene", None, None),
        P("gene", None),
    )
    out_specs = (P("gene", None, None), P("gene", None, None, None, None))
    return jax.shard_map(shards, mesh=mesh, in_specs=in_specs, out_specs=out_specs, check_vma=False)
```

```python
import functools

import jax
import jax.numpy as jnp
from jax import lax
from jax.experimental import pallas as pl
from jax.experimental.pallas import tpu as pltpu
from jax.sharding import PartitionSpec as P

ITERS = 2
STEP = 0.5
SHRINK = 0.02
TILE = 128
EXTRA = 16
BF = jnp.bfloat16
F32 = jnp.float32

ALL = (0, 1, -1, 2, -2, 3, -3, 4)
PARITY = (0, 2, -2, 4)
MASKS = tuple(
    4 * y + x
    for (x, y) in (
        (0, 0), (2, 2), (2, 0), (0, 2), (2, 1), (0, 3), (2, 3), (0, 1),
        (1, 0), (3, 2), (3, 0), (1, 2), (1, 1), (3, 3), (1, 3), (3, 1),
    )
)
PARTNER = 2


def order(backs):
    return tuple((back, other) for other in (0, 1) for back in backs)


VMEM = pl.BlockSpec(memory_space=pltpu.VMEM)
SMEM = pl.BlockSpec(memory_space=pltpu.SMEM)
ANY = pl.BlockSpec(memory_space=pl.ANY)
PARAMS = pltpu.CompilerParams(vmem_limit_bytes=16 * 1024 * 1024)


def shift_z(x, chips):
    count = lax.axis_size("sample")
    return lax.ppermute(x, "sample", [(i, (i + 2 * chips) % count) for i in range(count)])


def swap_core(x):
    count = lax.axis_size("sample")
    return lax.ppermute(x, "sample", [(i, i ^ 1) for i in range(count)])


def gather_shards(x, backs):
    own = [x] + [shift_z(x, back) for back in backs[1:]]
    return own + [swap_core(piece) for piece in own]


def forward_shards(x):
    up, down, up2, down2 = (shift_z(x, back) for back in (1, -1, 2, -2))
    half = x.shape[0] // 2
    far = jnp.concatenate([shift_z(up2[:half], 2), shift_z(down2[half:], -2)], axis=0)
    own = [x, up, down, up2, down2, shift_z(up2, 1), shift_z(down2, -1), far]
    return own + [swap_core(piece) for piece in own]


def swap_owner(x, sample_xor, gene_xor):
    samples, genes = lax.axis_size("sample"), lax.axis_size("gene")
    pairs = [
        (s * genes + g, (s ^ sample_xor) * genes + (g ^ gene_xor(s)))
        for s in range(samples)
        for g in range(genes)
    ]
    return lax.ppermute(x, ("sample", "gene"), pairs)


def dot(a, b):
    return jnp.dot(a, b, preferred_element_type=F32)


def dot_over_rows(a, b):
    return lax.dot_general(a, b, (((0,), (0,)), ((), ())), preferred_element_type=F32)


def column_of(cols_ref, counts_ref, h, p):
    live = jnp.where(p < counts_ref[0, h], cols_ref[0, h, p], 2)
    return jnp.where(h == lax.axis_index("gene"), p, live)


def pick_blocks(cols_ref, h, own, left, right):
    picks = [jnp.where(own, p, cols_ref[0, h, p]) for p in range(2)]
    return jnp.concatenate([jnp.where(pick == 1, right, left) for pick in picks], axis=-1)


def outgoing_kernel(cols_ref, x_ref, out_ref):
    left, right = x_ref[:, :TILE], x_ref[:, TILE:]
    for h in range(out_ref.shape[0]):
        out_ref[h] = pick_blocks(cols_ref, h, h == lax.axis_index("gene"), left, right)


def arrange_kernel(cols_ref, *refs):
    pieces, outs = refs[:-2], refs[-2:]
    g = lax.axis_index("gene")
    for owner, out_ref in zip(owners(), outs):
        for j, piece in enumerate(pieces):
            out_ref[j] = pick_blocks(cols_ref, g ^ mask_of(owner), owner == 0, piece[:, :TILE], piece[:, TILE:])


def mask_of(s):
    mask = s * 0
    for at, value in enumerate(MASKS):
        mask = jnp.where(s == at, value, mask)
    return mask


def owners():
    s = lax.axis_index("sample")
    return s, s ^ PARTNER


def placed(tiles, columns):
    zero = jnp.zeros((TILE, TILE), BF)
    rows = [
        jnp.concatenate([jnp.where(column == c, tile.astype(BF), zero) for c in range(2)], axis=1)
        for tile, column in zip(tiles, columns)
    ]
    return jnp.concatenate(rows, axis=0)


def first_columns_kernel(
    cols_ref, counts_ref, slots_ref, cross_ref, diag_ref, y_ref, tile_ref, hub_ref, sem
):
    s, g = lax.axis_index("sample"), lax.axis_index("gene")
    copy = pltpu.make_async_copy(diag_ref.at[pl.ds(0, 2)], hub_ref, sem)
    copy.start()
    total = jnp.zeros(y_ref.shape, F32)
    for h in range(cross_ref.shape[0]):
        columns = [jnp.where(h == g, 2, column_of(cols_ref, counts_ref, h, p)) for p in range(2)]
        total += dot(slots_ref[h], placed([cross_ref[h, p] for p in range(2)], columns))
    copy.wait()
    total += dot(slots_ref[g], placed([hub_ref[p] for p in range(2)], range(2)))
    y_ref[...] = total.astype(BF)
    for p in range(2):
        tile_ref[p] = jnp.where(s == 0, hub_ref[p], cross_ref[g ^ mask_of(s), p])


def position_of(j):
    back, other = order(ALL)[j]
    s = lax.axis_index("sample")
    chips = lax.axis_size("sample") // 2
    return lax.rem(s // 2 - back + chips, chips) * 2 + (s % 2 ^ other)


def peer_of(j):
    return lax.axis_index("gene") ^ mask_of(position_of(j))


def later_columns_kernel(cols_ref, counts_ref, slots_ref, *refs):
    pieces, y_ref = refs[:-1], refs[-1]
    total = jnp.zeros(y_ref.shape, F32)
    for j, piece in enumerate(pieces):
        h = peer_of(j)
        columns = [column_of(cols_ref, counts_ref, h, p) for p in range(2)]
        total += dot(slots_ref[h], placed([piece[p, :TILE] for p in range(2)], columns))
    y_ref[...] = total.astype(BF)


def gradient_kernel(cols_ref, counts_ref, own_rows_ref, partner_rows_ref, *refs):
    pieces, outs = refs[:-2], refs[-2:]
    g = lax.axis_index("gene")
    for owner, rows_ref, out_ref in zip(owners(), (own_rows_ref, partner_rows_ref), outs):
        total = jnp.zeros((2 * TILE, 2 * TILE), F32)
        for j, piece in enumerate(pieces):
            total += dot_over_rows(rows_ref[j], piece[...])
        for p in range(2):
            rows = total[p * TILE : (p + 1) * TILE]
            column = column_of(cols_ref, counts_ref, g ^ mask_of(owner), p)
            out_ref[p] = jnp.where(column == 1, rows[:, TILE:], rows[:, :TILE])


def proximal(tile, gradient, mirrored, diagonal, sample_total):
    symmetric = 0.5 * (gradient + mirrored.T) / sample_total
    stepped = tile - STEP * symmetric
    shrunk = jnp.where(
        stepped > 0, jnp.maximum(stepped - SHRINK, 0.0), jnp.minimum(stepped + SHRINK, 0.0)
    )
    barrier = 0.5 * (stepped + jnp.sqrt(stepped * stepped + 4.0 * STEP))
    return jnp.where(diagonal, barrier, shrunk)


def eye():
    shape = (TILE, TILE)
    return lax.broadcasted_iota(jnp.int32, shape, 0) == lax.broadcasted_iota(jnp.int32, shape, 1)


def step_kernel(sample_total, cols_ref, counts_ref, tile_ref, *refs):
    (own_ref, partner_ref, mirrored_ref, far_ref), riders = refs[:4], refs[4:-2]
    new_ref, low_ref = refs[-2:]
    s, g = lax.axis_index("sample"), lax.axis_index("gene")
    on_diagonal = jnp.where(s == 0, eye().astype(F32), 0.0) > 0.5
    for p in range(2):
        gradient, mirrored = own_ref[p] + partner_ref[p], mirrored_ref[p] + far_ref[p]
        new = proximal(tile_ref[p], gradient, mirrored, on_diagonal, sample_total)
        new = jnp.where(column_of(cols_ref, counts_ref, g ^ mask_of(s), p) < 2, new, 0.0)
        new_ref[p] = new
        low_ref[p, :TILE] = new.astype(BF)
        for rider in riders:
            low_ref[p, TILE:] = rider[p]


def upper(strict):
    shape = (TILE, TILE)
    row, column = lax.broadcasted_iota(jnp.int32, shape, 0), lax.broadcasted_iota(jnp.int32, shape, 1)
    return row < column if strict else row <= column


def chunk_at(s):
    return (s & 1) * 8 + (s & 2) * 2 + (s & 4) // 2 + (s & 8) // 8


def gram_kernel(x_ref, after_ref, keep_ref, send_ref, all_ref):
    here = chunk_at(lax.axis_index("sample"))
    half = keep_ref.shape[0]
    for b in range(2 * half):
        x = x_ref[:, 2 * b * TILE : 2 * (b + 1) * TILE]
        first, second = (dot_over_rows(x[:, at : at + TILE], x[:, at : at + TILE]) for at in (0, TILE))
        diagonal = jnp.sum(jnp.where(eye(), second, 0.0), axis=0, keepdims=True)
        at = chunk_at(b) ^ here
        all_ref[at, :TILE] = jnp.where(upper(False), first, second)
        all_ref[at, TILE:] = jnp.broadcast_to(diagonal, (EXTRA, TILE))
    keep_ref[...] = all_ref[:half]
    send_ref[...] = all_ref[half:].astype(BF)


def halve_kernel(kept_ref, received_ref, keep_ref, send_ref):
    half = keep_ref.shape[0]
    keep_ref[...] = kept_ref[:half] + received_ref[:half].astype(F32)
    send_ref[...] = (kept_ref[half:] + received_ref[half:].astype(F32)).astype(send_ref.dtype)


def diagonal_kernel(sample_total, kept_ref, received_ref, tiles_ref, out_ref, tile_ref, sem):
    first_tile = 2 * lax.axis_index("sample")
    copy = pltpu.make_async_copy(tiles_ref.at[pl.ds(first_tile, 2)], tile_ref, sem)
    copy.start()
    whole = kept_ref[0] + received_ref[0]
    packed = whole[:TILE]
    turned = packed.T
    first = jnp.where(upper(False), packed, turned)
    second = jnp.where(upper(True), turned, packed)
    second = jnp.where(eye(), whole[TILE : TILE + 1], second)
    copy.wait()
    for p, gram in enumerate((first, second)):
        high = gram.astype(BF)
        low = (gram - high.astype(F32)).astype(BF)
        tile = tile_ref[p]
        for _ in range(ITERS):
            lowered = tile.astype(BF)
            gradient = dot(high, lowered) + dot(low, lowered)
            tile = proximal(tile, gradient, gradient, eye(), sample_total)
        lowered = tile.astype(BF)
        rest = jnp.sum(jnp.where(eye(), tile - lowered.astype(F32), 0.0), axis=0, keepdims=True)
        out_ref[p, :TILE] = lowered
        out_ref[p, TILE:] = jnp.broadcast_to(rest, (EXTRA, TILE)).astype(BF)


def assemble_kernel(*refs):
    pieces, (cross_ref, diag_ref, cross_part, diag_part, cross_sems, diag_sems) = refs[:-6], refs[-6:]
    copies = []
    for j, piece in enumerate(pieces):
        at = position_of(j)
        for p in range(2):
            tile = piece[p, :TILE].astype(F32)
            rest = piece[p, 2 * TILE :].astype(F32)[:1]
            rider = piece[p, TILE : 2 * TILE].astype(F32) + jnp.where(eye(), rest, 0.0)
            cross_part[j, p] = jnp.where(at == 0, 0.0, tile)
            diag_part[j, p] = jnp.where(at == 0, tile, rider)
        copies += [
            pltpu.make_async_copy(cross_part.at[j], cross_ref.at[peer_of(j)], cross_sems.at[j]),
            pltpu.make_async_copy(diag_part.at[j], diag_ref.at[pl.ds(2 * at, 2)], diag_sems.at[j]),
        ]
        for copy in copies[-2:]:
            copy.start()
    for copy in copies:
        copy.wait()


def call(kernel, outs, spaces, *args, scratch=()):
    moved = sum(x.size * x.dtype.itemsize for x in list(args) + jax.tree.leaves(outs))
    return pl.pallas_call(
        kernel,
        out_shape=outs,
        in_specs=list(spaces) + [VMEM] * (len(args) - len(spaces)),
        out_specs=jax.tree.map(lambda _: VMEM, outs),
        compiler_params=PARAMS,
        scratch_shapes=scratch,
        cost_estimate=pl.CostEstimate(flops=10**8, bytes_accessed=moved, transcendentals=0),
    )(*args)


def shards(samples, diag_tiles, cross_tiles, peer_cols, pair_counts):
    s, g = lax.axis_index("sample"), lax.axis_index("gene")
    genes = lax.axis_size("gene")
    rows = samples.shape[0]
    sample_total = rows * lax.axis_size("sample")
    shape = jax.ShapeDtypeStruct
    cols, counts = peer_cols, pair_counts
    part = shape((rows, 2 * TILE), BF)

    hubs = samples[:, : 2 * TILE]
    outgoing = call(outgoing_kernel, shape((genes,) + part.shape, BF), [SMEM], cols, hubs)
    slots = lax.all_to_all(outgoing, "gene", split_axis=0, concat_axis=0, tiled=True)
    rows_shape = shape((len(order(PARITY)),) + part.shape, BF)
    arranged = call(arrange_kernel, [rows_shape] * 2, [SMEM], cols, *gather_shards(hubs, PARITY))
    own_rows = swap_owner(arranged[0], 0, lambda s: MASKS[s])
    partner_rows = swap_owner(arranged[1], 0, lambda s: MASKS[s ^ PARTNER])

    pair = (2, TILE, TILE)
    for iteration in range(ITERS):
        if iteration == 0:
            columns, tile = call(
                first_columns_kernel,
                [part, shape(pair, F32)],
                [SMEM, SMEM, VMEM, VMEM, ANY],
                cols, counts, slots, cross_tiles[0], diag_tiles,
                scratch=[pltpu.VMEM(pair, F32), pltpu.SemaphoreType.DMA(())],
            )
            chunk = (TILE + EXTRA, TILE)
            count = diag_tiles.shape[0] // 2
            kept, sent = call(
                gram_kernel,
                [shape((count // 2,) + chunk, F32), shape((count // 2,) + chunk, BF)],
                [VMEM, ANY],
                samples, columns,
                scratch=[pltpu.VMEM((count,) + chunk, F32)],
            )
            received = swap_core(sent)
            for bit, dtype in ((2, BF), (4, F32), (8, F32)):
                half = (kept.shape[0] // 2,) + chunk
                kept, sent = call(halve_kernel, [shape(half, F32), shape(half, dtype)], [], kept, received)
                received = lax.ppermute(sent, "sample", [(i, i ^ bit) for i in range(lax.axis_size("sample"))])
            my_diag = call(
                functools.partial(diagonal_kernel, sample_total),
                shape((2,) + chunk, BF),
                [VMEM, VMEM, ANY],
                kept, received, diag_tiles,
                scratch=[pltpu.VMEM((2, TILE, TILE), F32), pltpu.SemaphoreType.DMA(())],
            )
        else:
            columns = call(later_columns_kernel, part, [SMEM, SMEM], cols, counts, slots, *pieces)
        own, partner = call(
            gradient_kernel,
            [shape(pair, F32)] * 2,
            [SMEM, SMEM],
            cols, counts, own_rows, partner_rows, *gather_shards(columns, PARITY),
        )
        others = (
            swap_owner(partner, PARTNER, lambda s: 0),
            swap_owner(own, 0, lambda s: MASKS[s]),
            swap_owner(partner, PARTNER, lambda s: MASKS[s ^ PARTNER]),
        )
        riders = [my_diag] if iteration == ITERS - 1 else []
        tile, lowered = call(
            functools.partial(step_kernel, sample_total),
            [shape(pair, F32), shape((2, TILE + sum(r.shape[1] for r in riders), TILE), BF)],
            [SMEM, SMEM],
            cols, counts, tile, own, *others, *riders,
        )
        pieces = forward_shards(lowered)

    place = pl.BlockSpec(memory_space=pl.ANY)
    chunk = pltpu.VMEM((len(pieces),) + pair, F32)
    cross, diag = pl.pallas_call(
        assemble_kernel,
        out_shape=[shape(cross_tiles.shape[1:], F32), shape(diag_tiles.shape, F32)],
        in_specs=[VMEM] * len(pieces),
        out_specs=[place, place],
        scratch_shapes=[chunk, chunk] + [pltpu.SemaphoreType.DMA((len(pieces),))] * 2,
        compiler_params=PARAMS,
    )(*pieces)
    return diag, cross[None]


def solution(mesh):
    in_specs = (
        P("sample", "gene"),
        P("gene", None, None),
        P("gene", None, None, None, None),
        P("gene", None, None),
        P("gene", None),
    )
    out_specs = (P("gene", None, None), P("gene", None, None, None, None))
    return jax.shard_map(shards, mesh=mesh, in_specs=in_specs, out_specs=out_specs, check_vma=False)
```
